32 devices in a mesh: rep: 2 (over x), tp: 4 (over y, core), dp: 4 (over z).
Axes of the slice: x: 2, y: 2, z: 4, core: 2. Of those that a mesh axis runs over, the one named last changes fastest.
Arguments:
- patches: bfloat16 [2048, 3072], P(('rep', 'dp'), 'tp'), parts along dimension 0, may hold values from -6 to 6
- ordering: int32 [2048], P(('rep', 'dp')), parts along dimension 0, may hold values from 0 to 255, as said below
- w_in: bfloat16 [3072, 12288], P(None, 'tp'), may hold values from -0.109375 to 0.109375
- w_out: bfloat16 [12288, 3072], P('tp'), may hold values from -0.0546875 to 0.0546875
- cotangent: bfloat16 [2048, 3072], P(('rep', 'dp'), 'tp'), parts along dimension 0, may hold values from -1.5 to 1.5
Outputs:
- mixed: bfloat16 [2048, 3072], P(('rep', 'dp'), 'tp'), parts along dimension 0
- grad_patches: bfloat16 [2048, 3072], P(('rep', 'dp'), 'tp'), parts along dimension 0
- grad_in: float32 [6144, 12288], P(('rep', 'dp'), 'tp'), parts along dimension 0
- grad_out: float32 [24576, 3072], P(('rep', 'tp'), 'dp'), parts along dimension 0
The draws below stay inside these ranges and needn't reach their ends.
There are 2 independent parts, one for each index of `rep`. The reference program is written for one: setup_inputs(seed, part) draws one part's arguments, and reference() takes and returns one part's arrays. A program takes and returns all parts, laid end to end along the dimension named above; an argument that names none is the same for every part. Nothing has to cross between parts.
Inputs may be any that keep to these rules, and one draw needn't show every extreme that they name: `ordering`: each block of 256 consecutive entries (one group) lists every number from 0 to 255 once; entry k of a block names the patch of sorted row k, whose level is k // 64.
All inputs are finite; a program needn't handle non-finite values.
Results may differ from the reference program's by a relative error of at most 0.0095.
Values may be sent and summed in bfloat16 or wider, within the bound.
No kernel may reach another device: no remote copies, remote signals or barrier semaphores. Data moves between devices by JAX's collectives and lax.ppermute only.
A program may use at most 256 MiB of HBM per device.

```python
import jax
import jax.numpy as jnp
from jax import lax

D = 3072
FF = 12288
LEVEL_ROWS = 64
PATCHES = 1024
N_DP = 4


def draw_ordering(key, part):
    key = jax.random.fold_in(key, 11)
    group_rows = 4 * LEVEL_ROWS
    subkeys = jax.random.split(key, N_DP)
    shuffled = jax.vmap(lambda one_key: jax.random.permutation(one_key, group_rows))(subkeys)
    return shuffled.reshape(N_DP * group_rows).astype(jnp.int32)


def with_spikes(array, key, source, target, parts, factor):
    def block_of(axis_at):
        return (jnp.arange(array.shape[axis_at]) // (array.shape[axis_at] // parts)).reshape((-1,) + (1,) * (array.ndim - 1 - axis_at))

    one_side = jax.random.permutation(key, parts)[block_of(target)]
    other_side = (block_of(target) + parts // 2) % parts
    return jnp.where((block_of(source) == one_side) | (block_of(source) == other_side), factor * array, array)


def block_levels(own_key, extent, shards, smallest, largest):
    loudness, own = 1.0, jax.random.fold_in(own_key, 6)
    for dim, parts in shards:
        heights = jnp.exp(jax.random.uniform(jax.random.fold_in(own, dim), (parts,), jnp.float32, smallest / len(shards), largest / len(shards)))
        loudness = loudness * jnp.repeat(heights, extent[dim] // parts).reshape([-1 if axis == dim else 1 for axis in range(len(extent))])
    return loudness


def gaussian(rng, dims, width, most, shards=(), held_as=jnp.bfloat16):
    gain = block_levels(rng, dims, shards, -0.22, 0.18) if shards else 1.0
    entries = jax.random.normal(rng, dims, jnp.float32) * width * gain
    return jnp.minimum(jnp.maximum(entries, -most), most).astype(held_as)


def noise_with(stream_key, shape, width, limit, shards, heavy, kind=jnp.bfloat16):
    array = width * jax.random.normal(stream_key, shape, jnp.float32)
    if shards:
        array = array * block_levels(stream_key, shape, shards, -0.22, 0.18)
    return jnp.clip(with_spikes(array, jax.random.fold_in(stream_key, 3), *heavy), -limit, limit).astype(kind)


def setup_inputs(seed: int = 0, part: int = 0) -> dict:
    streams_of = jax.random.split(jax.random.key(seed), 6)
    part_splits = jax.random.split(jax.random.fold_in(streams_of[5], part), 6)
    return {
        "patches": noise_with(part_splits[0], (PATCHES, D), 1.0, 6.0, ((0, 4), (1, 4)), (0, 1, 4, 2.0)),
        "ordering": draw_ordering(jax.random.fold_in(jax.random.fold_in(streams_of[5], part), 71), part),
        "w_in": gaussian(streams_of[2], (D, FF), D ** -0.5, 0.109375, ((1, 4),)),
        "w_out": gaussian(streams_of[3], (FF, D), FF ** -0.5, 0.0546875, ((0, 4),)),
        "cotangent": noise_with(part_splits[4], (PATCHES, D), 0.25, 1.5, ((0, 4), (1, 4)), (0, 1, 4, 2.0)),
    }


def gelu_slope(pre_act):
    return jax.jvp(jax.nn.gelu, (pre_act,), (jnp.ones_like(pre_act),))[1]


def reference(patches, ordering, w_in, w_out, cotangent):
    group_rows = 4 * LEVEL_ROWS
    x_groups = patches.reshape(N_DP, group_rows, D)
    o_groups = ordering.reshape(N_DP, group_rows)
    c_groups = cotangent.reshape(N_DP, group_rows, D)

    def one_group(totals, group_items):
        x_group, o_group, c_group = group_items
        rows_sorted = jnp.take(x_group, o_group, axis=0)
        cot_sorted = jnp.take(c_group, o_group, axis=0)
        out_blocks = []
        back_blocks = []
        term_in = jnp.zeros((D, FF), jnp.float32)
        term_out = jnp.zeros((FF, D), jnp.float32)
        for level_idx in range(4):
            prefix_end = FF >> level_idx
            first_row = level_idx * LEVEL_ROWS
            rows_part = rows_sorted[first_row:first_row + LEVEL_ROWS]
            cot_part = cot_sorted[first_row:first_row + LEVEL_ROWS]
            w_first = w_in[:, :prefix_end]
            w_second = w_out[:prefix_end]
            pre_act = jnp.dot(rows_part, w_first, preferred_element_type=jnp.float32)
            hidden = jax.nn.gelu(pre_act).astype(jnp.bfloat16)
            out_blocks.append(jnp.dot(hidden, w_second, preferred_element_type=jnp.float32))
            back_hidden = jnp.dot(cot_part, w_second.T, preferred_element_type=jnp.float32)
            back_pre = (back_hidden * gelu_slope(pre_act)).astype(jnp.bfloat16)
            back_blocks.append(jnp.dot(back_pre, w_first.T, preferred_element_type=jnp.float32))
            term_in = term_in.at[:, :prefix_end].add(jnp.dot(rows_part.T, back_pre, preferred_element_type=jnp.float32))
            term_out = term_out.at[:prefix_end].add(jnp.dot(hidden.T, cot_part, preferred_element_type=jnp.float32))
        inverse = jnp.zeros((group_rows,), jnp.int32).at[o_group].set(jnp.arange(group_rows, dtype=jnp.int32))
        mixed_group = jnp.take(jnp.concatenate(out_blocks, axis=0), inverse, axis=0).astype(jnp.bfloat16)
        grad_group = jnp.take(jnp.concatenate(back_blocks, axis=0), inverse, axis=0).astype(jnp.bfloat16)
        rounded_in = lax.optimization_barrier(term_in.astype(jnp.bfloat16)).astype(jnp.float32)
        rounded_out = lax.optimization_barrier(term_out.astype(jnp.bfloat16)).astype(jnp.float32)
        return (totals[0] + rounded_in, totals[1] + rounded_out), (mixed_group, grad_group)

    start_totals = (jnp.zeros((D, FF), jnp.float32), jnp.zeros((FF, D), jnp.float32))
    totals, results = lax.scan(one_group, start_totals, (x_groups, o_groups, c_groups))
    mixed = results[0].reshape(N_DP * group_rows, D)
    grad_patches = results[1].reshape(N_DP * group_rows, D)
    return (mixed, grad_patches, totals[0], totals[1])
```

```python
import functools
import math

import jax
import jax.numpy as jnp
from jax import lax
from jax.experimental import pallas as pl
from jax.experimental.pallas import tpu as pltpu
from jax.sharding import PartitionSpec as P

LEVELS = 4
VMEM_BYTES = 60 * 1024 * 1024
ROOT = math.sqrt(2.0 / math.pi)


def contract_cols(left_side, right_side):
    return lax.dot_general(
        left_side, right_side, (((1,), (1,)), ((), ())), preferred_element_type=jnp.float32
    )


def contract_rows(left_side, right_side):
    return lax.dot_general(
        left_side, right_side, (((0,), (0,)), ((), ())), preferred_element_type=jnp.float32
    )


def gelu_and_slope(pre_act):
    square = pre_act * pre_act
    tanh = jnp.tanh(ROOT * pre_act * (1.0 + 0.044715 * square))
    half = 0.5 * (1.0 + tanh)
    slope = half + 0.5 * pre_act * (1.0 - tanh * tanh) * (ROOT * (1.0 + 0.134145 * square))
    return pre_act * half, slope


def fill(meta, blocks, x_full, c_full):
    rows = x_full.shape[0]
    for spot, block in enumerate(blocks):
        width = block.shape[1]
        at = pl.ds(pl.multiple_of(meta[3 + spot], 128), width)
        x_full[:, at] = block[:rows, :]
        c_full[:, at] = block[rows:, :]


def own_columns(meta, x_full, c_full, x_cols, c_cols):
    at = pl.ds(pl.multiple_of(meta[2], 128), x_cols.shape[1])
    x_cols[...] = x_full[:, at]
    c_cols[...] = c_full[:, at]


def activations(meta, x_full, c_full, w_first, w_second):
    rows = x_full.shape[0]
    units = w_first.shape[1]
    pre_act = jnp.dot(x_full[...], w_first[...], preferred_element_type=jnp.float32)
    back_hidden = contract_cols(c_full[...], w_second[...])
    hidden, slope = gelu_and_slope(pre_act)
    unit_ids = meta[0] + pl.program_id(0) * units + lax.broadcasted_iota(jnp.int32, (rows, units), 1)
    row_ids = lax.broadcasted_iota(jnp.int32, (rows, units), 0)
    keep = unit_ids < lax.shift_right_logical(meta[1], row_ids // (rows // LEVELS))
    hidden = jnp.where(keep, hidden, 0.0).astype(jnp.bfloat16)
    back_pre = jnp.where(keep, back_hidden * slope, 0.0).astype(jnp.bfloat16)
    return hidden, back_pre


def home_kernel(count, meta, *refs):
    blocks, (w_first, w_second) = refs[:count], refs[count : count + 2]
    parts, hidden_out, back_out, x_cols, c_cols, x_full, c_full, total_out, total_in = refs[count + 2 :]
    step = pl.program_id(0)
    rows = x_full.shape[0]

    @pl.when(step == 0)
    def _():
        fill(meta, blocks, x_full, c_full)
        own_columns(meta, x_full, c_full, x_cols, c_cols)

    hidden, back_pre = activations(meta, x_full, c_full, w_first, w_second)
    hidden_out[...] = hidden
    back_out[...] = back_pre
    share_out = jnp.dot(hidden, w_second[...], preferred_element_type=jnp.float32)
    share_in = contract_cols(back_pre, w_first[...])

    @pl.when(step == 0)
    def _():
        total_out[...] = share_out
        total_in[...] = share_in

    @pl.when(step > 0)
    def _():
        total_out[...] += share_out
        total_in[...] += share_in

    @pl.when(step == pl.num_programs(0) - 1)
    def _():
        for spot, block in enumerate(blocks):
            at = pl.ds(pl.multiple_of(meta[3 + spot], 128), block.shape[1])
            parts[spot, :rows, :] = total_out[:, at].astype(jnp.bfloat16)
            parts[spot, rows:, :] = total_in[:, at].astype(jnp.bfloat16)


def away_kernel(count, meta, *refs):
    blocks, (w_first, w_second) = refs[:count], refs[count : count + 2]
    hidden_out, back_out, x_cols, c_cols, x_full, c_full = refs[count + 2 :]

    @pl.when(pl.program_id(0) == 0)
    def _():
        fill(meta, blocks, x_full, c_full)
        own_columns(meta, x_full, c_full, x_cols, c_cols)

    hidden, back_pre = activations(meta, x_full, c_full, w_first, w_second)
    hidden_out[...] = hidden
    back_out[...] = back_pre


def last_kernel(count, others, meta, *refs):
    blocks, (w_first, w_second) = refs[:count], refs[count : count + 2]
    refs = refs[count + 2 :]
    past = [refs[4 * spot : 4 * spot + 4] for spot in range(others)]
    grad_in, grad_out, x_full, c_full, x_turned, c_all, hidden_all, back_all = refs[4 * others :]
    rows = x_full.shape[0]
    own = pl.ds(others * rows, rows)

    @pl.when(pl.program_id(0) == 0)
    def _():
        fill(meta, blocks, x_full, c_full)
        at = pl.ds(pl.multiple_of(meta[2], 128), c_all.shape[1])
        for spot in range(others):
            x_turned[:, pl.ds(spot * rows, rows)] = past[spot][2][...].T
            c_all[pl.ds(spot * rows, rows), :] = past[spot][3][...]
        x_turned[:, own] = x_full[:, at].T
        c_all[own, :] = c_full[:, at]

    hidden, back_pre = activations(meta, x_full, c_full, w_first, w_second)
    for spot in range(others):
        hidden_all[pl.ds(spot * rows, rows), :] = past[spot][0][...]
        back_all[pl.ds(spot * rows, rows), :] = past[spot][1][...]
    hidden_all[own, :] = hidden
    back_all[own, :] = back_pre
    grad_in[...] = jnp.dot(x_turned[...], back_all[...], preferred_element_type=jnp.float32)
    grad_out[...] = contract_rows(hidden_all[...], c_all[...])


def whole_spec(shape):
    zeros = (0,) * len(shape)
    return pl.BlockSpec(shape, lambda step, meta: zeros)


def unit_block(units):
    for size in (512, 384, 256, 128):
        if units % size == 0:
            return size
    return units


def run_kernel(kernel, meta, whole_in, unit_cols_in, w_in, w_out, outs, scratch, flops, order):
    units = w_in.shape[1]
    size = unit_block(units)
    cols = lambda rows: pl.BlockSpec((rows, size), lambda step, meta: (0, step))
    by_rows = lambda width: pl.BlockSpec((size, width), lambda step, meta: (step, 0))
    inputs, in_specs = [], []
    for kind, array in order:
        inputs.append(array)
        if kind == "whole":
            in_specs.append(whole_spec(array.shape))
        elif kind == "cols":
            in_specs.append(cols(array.shape[0]))
        else:
            in_specs.append(by_rows(array.shape[1]))
    out_specs = [
        whole_spec(shape) if kind == "whole" else cols(shape[0]) if kind == "cols" else by_rows(shape[1])
        for shape, _, kind in outs
    ]
    moved = sum(array.size * array.dtype.itemsize for array in inputs)
    moved += sum(math.prod(shape) * jnp.dtype(dtype).itemsize for shape, dtype, _ in outs)
    return pl.pallas_call(
        kernel,
        out_shape=[jax.ShapeDtypeStruct(shape, dtype) for shape, dtype, _ in outs],
        grid_spec=pltpu.PrefetchScalarGridSpec(
            num_scalar_prefetch=1,
            grid=(units // size,),
            in_specs=in_specs,
            out_specs=out_specs,
            scratch_shapes=scratch,
        ),
        compiler_params=pltpu.CompilerParams(
            dimension_semantics=("arbitrary",), vmem_limit_bytes=VMEM_BYTES
        ),
        cost_estimate=pl.CostEstimate(flops=flops, bytes_accessed=moved, transcendentals=0),
    )(meta, *inputs)


def home_pass(meta, blocks, w_in, w_out, n_dp):
    rows2, width = blocks[0].shape
    rows, (model, units) = rows2 // 2, w_in.shape
    own = model // n_dp
    order = [("whole", block) for block in blocks] + [("cols", w_in), ("rows", w_out)]
    bf16 = jnp.bfloat16
    return run_kernel(
        functools.partial(home_kernel, len(blocks)), meta, None, None, w_in, w_out,
        [
            ((len(blocks), rows2, width), bf16, "whole"),
            ((rows, units), bf16, "cols"),
            ((rows, units), bf16, "cols"),
            ((rows, own), bf16, "whole"),
            ((rows, own), bf16, "whole"),
        ],
        [pltpu.VMEM((rows, model), bf16)] * 2 + [pltpu.VMEM((rows, model), jnp.float32)] * 2,
        8 * rows * model * units,
        order,
    )


def away_pass(meta, blocks, w_in, w_out, n_dp):
    rows, (model, units) = blocks[0].shape[0] // 2, w_in.shape
    own = model // n_dp
    order = [("whole", block) for block in blocks] + [("cols", w_in), ("rows", w_out)]
    bf16 = jnp.bfloat16
    return run_kernel(
        functools.partial(away_kernel, len(blocks)), meta, None, None, w_in, w_out,
        [
            ((rows, units), bf16, "cols"),
            ((rows, units), bf16, "cols"),
            ((rows, own), bf16, "whole"),
            ((rows, own), bf16, "whole"),
        ],
        [pltpu.VMEM((rows, model), bf16)] * 2,
        4 * rows * model * units,
        order,
    )


def last_pass(meta, blocks, past, w_in, w_out, n_dp):
    rows, (model, units) = blocks[0].shape[0] // 2, w_in.shape
    own = model // n_dp
    size = unit_block(units)
    everyone = rows * (len(past) + 1)
    order = [("whole", block) for block in blocks] + [("cols", w_in), ("rows", w_out)]
    for hidden, back_pre, x_cols, c_cols in past:
        order += [("cols", hidden), ("cols", back_pre), ("whole", x_cols), ("whole", c_cols)]
    bf16 = jnp.bfloat16
    return run_kernel(
        functools.partial(last_kernel, len(blocks), len(past)), meta, None, None, w_in, w_out,
        [((own, units), jnp.float32, "cols"), ((units, own), jnp.float32, "rows")],
        [
            pltpu.VMEM((rows, model), bf16),
            pltpu.VMEM((rows, model), bf16),
            pltpu.VMEM((own, everyone), bf16),
            pltpu.VMEM((everyone, own), bf16),
            pltpu.VMEM((everyone, size), bf16),
            pltpu.VMEM((everyone, size), bf16),
        ],
        4 * rows * model * units + 4 * everyone * own * units,
        order,
    )


def shards(patches, ordering, w_in, w_out, cotangent):
    n_tp, n_dp = lax.axis_size("tp"), lax.axis_size("dp")
    tp_rank, dp_rank = lax.axis_index("tp"), lax.axis_index("dp")
    rows, width = patches.shape
    model, units = w_in.shape
    paired = n_tp == 4

    def across(array, bits):
        return lax.ppermute(array, "tp", [(rank, rank ^ bits) for rank in range(n_tp)])

    def onward(array):
        return lax.ppermute(array, "dp", [(rank, (rank + 1) % n_dp) for rank in range(n_dp)])

    def spread(chunk):
        if not paired:
            return [lax.all_gather(chunk, "tp", axis=1, tiled=True)]
        opposite = across(chunk, 2)
        return [chunk, across(chunk, 1), opposite, across(opposite, 1)]

    offsets = [tp_rank ^ spot for spot in range(4)] if paired else [0]
    meta = jnp.stack(
        [tp_rank * units, jnp.int32(units * n_tp), dp_rank * (model // n_dp)]
        + [jnp.int32(offset * width) for offset in offsets]
    ).astype(jnp.int32)

    pick = (ordering[:, None] == jnp.arange(rows, dtype=jnp.int32)[None, :]).astype(jnp.bfloat16)
    place = lambda array: jnp.dot(pick, array, preferred_element_type=jnp.float32).astype(jnp.bfloat16)
    chunk = jnp.concatenate([place(patches), place(cotangent)], axis=0)

    parts, *kept = home_pass(meta, spread(chunk), w_in, w_out, n_dp)
    past = [kept]
    for step in range(1, n_dp):
        chunk = onward(chunk)
        blocks = spread(chunk)
        if step < n_dp - 1:
            past.append(away_pass(meta, blocks, w_in, w_out, n_dp))
        else:
            grad_in, grad_out = last_pass(meta, blocks, past, w_in, w_out, n_dp)

    if paired:
        far = across(parts[3], 1).astype(jnp.float32) + parts[2].astype(jnp.float32)
        near = across(parts[1], 1).astype(jnp.float32) + parts[0].astype(jnp.float32)
        summed = near + across(far.astype(jnp.bfloat16), 2).astype(jnp.float32)
    else:
        summed = lax.psum_scatter(parts[0], "tp", scatter_dimension=1, tiled=True)
    summed = summed.astype(jnp.bfloat16)
    put_back = lambda array: contract_rows(pick, array).astype(jnp.bfloat16)
    return (put_back(summed[:rows]), put_back(summed[rows:]), grad_in, grad_out)


def solution(mesh):
    return jax.shard_map(
        shards,
        mesh=mesh,
        in_specs=(
            P(("rep", "dp"), "tp"),
            P(("rep", "dp")),
            P(None, "tp"),
            P("tp", None),
            P(("rep", "dp"), "tp"),
        ),
        out_specs=(
            P(("rep", "dp"), "tp"),
            P(("rep", "dp"), "tp"),
            P(("rep", "dp"), "tp"),
            P(("rep", "tp"), "dp"),
        ),
        check_vma=False,
    )
```

```python
import functools
import math

import jax
import jax.numpy as jnp
from jax import lax
from jax.experimental import pallas as pl
from jax.experimental.pallas import tpu as pltpu
from jax.sharding import PartitionSpec as P

LEVELS = 4
MIB = 1024 * 1024
LIM = 23
FIXED = 5
ROOT = math.sqrt(2.0 / math.pi)


def contract_cols(left_side, right_side):
    return lax.dot_general(
        left_side, right_side, (((1,), (1,)), ((), ())), preferred_element_type=jnp.float32
    )


def contract_rows(left_side, right_side):
    return lax.dot_general(
        left_side, right_side, (((0,), (0,)), ((), ())), preferred_element_type=jnp.float32
    )


def gelu_and_slope(pre_act):
    square = pre_act * pre_act
    tanh = jnp.tanh(ROOT * pre_act * (1.0 + 0.044715 * square))
    half = 0.5 * (1.0 + tanh)
    slope = half + 0.5 * pre_act * (1.0 - tanh * tanh) * (ROOT * (1.0 + 0.134145 * square))
    return pre_act * half, slope


def unpack(pieces, at, x_out, c_out, to):
    level = x_out.shape[0] // LEVELS
    first = 0
    for piece in pieces:
        for start in range(0, piece.shape[0], 2 * level):
            x_out[first : first + level, to] = piece[start : start + level, at]
            c_out[first : first + level, to] = piece[start + level : start + 2 * level, at]
            first += level


def fill(meta, blocks, x_full, c_full, base=0, spots=None):
    for spot, pieces in enumerate(blocks):
        if spots is None or spot in spots:
            to = pl.ds(pl.multiple_of(meta[FIXED + spot] - base, 128), pieces[0].shape[1])
            unpack(pieces, slice(None), x_full, c_full, to)


def fill_late(meta, begun, blocks, x_full, c_full):
    if begun:
        fill(meta, blocks, x_full, c_full, meta[4], (2, 3))
    else:
        fill(meta, blocks, x_full, c_full)


def own_columns(meta, blocks, x_cols, c_cols):
    width = x_cols.shape[1]
    start = meta[2] * width
    for spot, pieces in enumerate(blocks):
        wide = pieces[0].shape[1]
        begin = meta[FIXED + spot]

        @pl.when((start >= begin) & (start < begin + wide))
        def _():
            at = pl.ds(pl.multiple_of(start - begin, 128), width) if width < wide else slice(None)
            unpack(pieces, at, x_cols, c_cols, slice(None))


def unit_slice(size, first=0):
    return pl.ds(pl.multiple_of(first + pl.program_id(0) * size, 128), size)


def views(weights):
    if len(weights) == 1:
        half = weights[0].shape[0] // 2
        return weights[0].at[pl.ds(0, half), :], weights[0].at[pl.ds(half, half), :]
    return weights


def products(x_full, c_full, first, weights, units):
    w_first, w_second = weights
    deep = pl.ds(first if isinstance(first, int) else pl.multiple_of(first, 128), x_full.shape[1])
    at = unit_slice(units)
    pre_act = jnp.dot(x_full[...], w_first[deep, at], preferred_element_type=jnp.float32)
    return pre_act, contract_cols(c_full[...], w_second[at, deep])


def activations(meta, pre_act, back_hidden):
    rows, units = pre_act.shape
    hidden, slope = gelu_and_slope(pre_act)
    back_pre = back_hidden * slope
    level = rows // LEVELS
    unit_ids = meta[0] + pl.program_id(0) * units + lax.broadcasted_iota(jnp.int32, (level, units), 1)
    keep = [unit_ids < lax.shift_right_logical(meta[1], level_idx) for level_idx in range(LEVELS)]
    cut = lambda array: jnp.concatenate(
        [
            jnp.where(keep[level_idx], array[level_idx * level : (level_idx + 1) * level], 0.0)
            for level_idx in range(LEVELS)
        ],
        axis=0,
    ).astype(jnp.bfloat16)
    return cut(hidden), cut(back_pre)


def sort_kernel(ordering, patches, cotangent, chunk):
    rows = patches.shape[0]
    level = rows // LEVELS
    patch_ids = lax.broadcasted_iota(jnp.int32, (rows, rows), 0)
    pick = (patch_ids == ordering[...]).astype(jnp.float32).astype(jnp.bfloat16)
    for spot, array in enumerate((patches, cotangent)):
        placed = contract_rows(pick, array[...]).astype(jnp.bfloat16)
        for level_idx in range(LEVELS):
            start = (2 * level_idx + spot) * level
            chunk[start : start + level, :] = placed[level_idx * level : (level_idx + 1) * level]


def restore_kernel(count, ordering, *refs):
    shares, (mixed, grad_patches) = refs[:count], refs[count:]
    rows = mixed.shape[0]
    level = rows // LEVELS
    total = sum(share[...].astype(jnp.float32) for share in shares).astype(jnp.bfloat16)
    patch_ids = lax.broadcasted_iota(jnp.int32, (rows, rows), 0)
    pick = (patch_ids == ordering[...]).astype(jnp.float32).astype(jnp.bfloat16)
    for spot, out in enumerate((mixed, grad_patches)):
        placed = jnp.concatenate(
            [total[(2 * idx + spot) * level : (2 * idx + spot + 1) * level] for idx in range(LEVELS)], axis=0
        )
        out[...] = jnp.dot(pick, placed, preferred_element_type=jnp.float32).astype(jnp.bfloat16)


def split_refs(refs, counts):
    groups = []
    for count in counts:
        groups.append(refs[:count])
        refs = refs[count:]
    return groups, refs


def open_kernel(counts, meta, *refs):
    blocks, (w_in, w_out, weights, pre_out, back_out, x_full, c_full, arrived) = split_refs(refs, counts)
    model, units = w_in.shape[0], pre_out.shape[1]

    def copies(step):
        cols = pl.ds(pl.multiple_of(step * units, 128), units)
        rows = pl.ds(pl.multiple_of(model + step * units, 128), units)
        return (
            pltpu.make_async_copy(w_in.at[:, cols], weights.at[pl.ds(0, model), cols], arrived.at[0, step]),
            pltpu.make_async_copy(w_out.at[cols, :], weights.at[rows, :], arrived.at[1, step]),
        )

    @pl.when(pl.program_id(0) == 0)
    def _():
        for step in range(w_in.shape[1] // units):
            for copy in copies(step):
                copy.start()
        fill(meta, blocks, x_full, c_full, meta[3])

    for copy in copies(pl.program_id(0)):
        copy.wait()
    pre_out[...], back_out[...] = products(x_full, c_full, meta[3], views([weights]), units)


def begin_kernel(counts, held, meta, *refs):
    blocks, refs = split_refs(refs, counts)
    weights, (pre_out, back_out, x_full, c_full) = refs[:held], refs[held:]

    @pl.when(pl.program_id(0) == 0)
    def _():
        fill(meta, blocks, x_full, c_full, meta[3])

    pre_out[...], back_out[...] = products(x_full, c_full, meta[3], views(weights), pre_out.shape[1])


def home_kernel(counts, held, begun, meta, *refs):
    blocks, refs = split_refs(refs, counts)
    (weights, begun, parts), refs = split_refs(refs, (held, begun, len(counts)))
    hidden_out, back_out, x_cols, c_cols, x_full, c_full, total_out, total_in = refs
    step = pl.program_id(0)
    rows, units = hidden_out.shape
    model = total_out.shape[1]
    level = rows // LEVELS

    @pl.when(step == 0)
    def _():
        fill_late(meta, begun, blocks, x_full, c_full)
        own_columns(meta, blocks, x_cols, c_cols)

    hidden, back_pre = late_products(meta, x_full, c_full, begun, weights, units)
    hidden_out[...] = hidden
    back_out[...] = back_pre
    w_first, w_second = views(weights)
    at = unit_slice(units)
    wide = model // 4
    shares = lambda cols: (
        jnp.dot(hidden, w_second[at, cols], preferred_element_type=jnp.float32),
        contract_cols(back_pre, w_first[cols, at]),
    )

    @pl.when(step == 0)
    def _():
        for first in range(0, model, wide):
            cols = pl.ds(first, wide)
            total_out[:, cols], total_in[:, cols] = shares(cols)

    @pl.when(step > 0)
    def _():
        for first in range(0, model, wide):
            cols = pl.ds(first, wide)
            more_out, more_in = shares(cols)
            total_out[:, cols] += more_out
            total_in[:, cols] += more_in

    @pl.when(step == pl.num_programs(0) - 1)
    def _():
        for spot, part in enumerate(parts):
            cols = pl.ds(pl.multiple_of(meta[FIXED + spot], 128), part.shape[1])
            for level_idx in range(LEVELS):
                here = pl.ds(level_idx * level, level)
                start = 2 * level_idx * level
                part[start : start + level, :] = total_out[here, cols].astype(jnp.bfloat16)
                part[start + level : start + 2 * level, :] = total_in[here, cols].astype(jnp.bfloat16)


def late_products(meta, x_full, c_full, begun, weights, units):
    if not begun:
        return activations(meta, *products(x_full, c_full, 0, views(weights), units))
    pre_act, back_hidden = products(x_full, c_full, meta[4], views(weights), units)
    return activations(meta, pre_act + begun[0][...], back_hidden + begun[1][...])


def away_kernel(counts, held, meta, *refs):
    blocks, refs = split_refs(refs, counts)
    weights, (hidden_out, back_out, x_cols, c_cols, x_full, c_full) = refs[:held], refs[held:]

    @pl.when(pl.program_id(0) == 0)
    def _():
        fill(meta, blocks, x_full, c_full)
        own_columns(meta, blocks, x_cols, c_cols)

    hidden_out[...], back_out[...] = late_products(meta, x_full, c_full, (), weights, hidden_out.shape[1])


def last_kernel(counts, held, begun, others, meta, *refs):
    blocks, refs = split_refs(refs, counts)
    (weights, begun, *past), refs = split_refs(refs, (held, begun) + (4,) * others)
    grad_in, grad_out, x_full, c_full, x_cols, x_turned, c_all, hidden_all, back_all = refs
    rows = x_full.shape[0]
    own = pl.ds(others * rows, rows)

    @pl.when(pl.program_id(0) == 0)
    def _():
        for spot in range(others):
            x_turned[:, pl.ds(spot * rows, rows)] = past[spot][2][...].T
            c_all[pl.ds(spot * rows, rows), :] = past[spot][3][...]
        fill_late(meta, begun, blocks, x_full, c_full)
        own_columns(meta, blocks, x_cols, c_all.at[own, :])
        x_turned[:, own] = x_cols[...].T

    hidden, back_pre = late_products(meta, x_full, c_full, begun, weights, hidden_all.shape[1])
    for spot in range(others):
        hidden_all[pl.ds(spot * rows, rows), :] = past[spot][0][...]
        back_all[pl.ds(spot * rows, rows), :] = past[spot][1][...]
    hidden_all[own, :] = hidden
    back_all[own, :] = back_pre
    grad_in[...] = jnp.dot(x_turned[...], back_all[...], preferred_element_type=jnp.float32)
    grad_out[...] = contract_rows(hidden_all[...], c_all[...])


def unit_block(units, most):
    for size in (768, 512, 384, 256, 128):
        if size <= most and units % size == 0:
            return size
    return units


def run_kernel(kernel, name, meta, size, units, inputs, outs, scratch, flops, limit):
    def spec(shape, kind):
        zeros = (0,) * len(shape)
        if kind == "whole":
            return pl.BlockSpec(shape, lambda step, meta: zeros, pipeline_mode=pl.Buffered(1))
        if kind == "cols":
            return pl.BlockSpec((shape[0], size), lambda step, meta: (0, step))
        if kind == "rows":
            return pl.BlockSpec((size, shape[1]), lambda step, meta: (step, 0))
        return pl.BlockSpec(memory_space=pltpu.VMEM if kind == "vmem" else pl.ANY)

    resident = lambda array, kind: pltpu.with_memory_space_constraint(array, pltpu.VMEM if kind == "vmem" else pltpu.HBM)
    shape_of = lambda shape, dtype, kind: (
        pltpu.VMEM(shape, dtype) if kind == "vmem" else jax.ShapeDtypeStruct(shape, dtype)
    )
    moved = sum(array.size * array.dtype.itemsize for array, kind in inputs if kind != "vmem")
    moved += sum(math.prod(shape) * jnp.dtype(dtype).itemsize for shape, dtype, kind in outs if kind != "vmem")
    return pl.pallas_call(
        kernel,
        name=name,
        out_shape=[shape_of(*out) for out in outs],
        grid_spec=pltpu.PrefetchScalarGridSpec(
            num_scalar_prefetch=1,
            grid=(units // size,),
            in_specs=[spec(array.shape, kind) for array, kind in inputs],
            out_specs=[spec(shape, kind) for shape, _, kind in outs],
            scratch_shapes=scratch,
        ),
        compiler_params=pltpu.CompilerParams(dimension_semantics=("arbitrary",), vmem_limit_bytes=limit * MIB),
        cost_estimate=pl.CostEstimate(flops=flops, bytes_accessed=moved, transcendentals=0),
    )(meta, *[resident(*pair) for pair in inputs])


def shards(patches, ordering, w_in, w_out, cotangent):
    n_tp, n_dp = lax.axis_size("tp"), lax.axis_size("dp")
    tp_rank, dp_rank = lax.axis_index("tp"), lax.axis_index("dp")
    rows, width = patches.shape
    model, units = w_in.shape
    own = model // n_dp
    bf16, f32 = jnp.bfloat16, jnp.float32
    paired = n_tp == 4 and model == units
    swap = lambda bits: [(rank, rank ^ bits) for rank in range(n_tp)]
    cross = lambda array, pairs: lax.ppermute(array, "tp", pairs)
    onward = lambda array: lax.ppermute(array, "dp", [(rank, (rank + 1) % n_dp) for rank in range(n_dp)])
    after = lambda array, done: lax.optimization_barrier((array, done))[0]

    def near_of(chunk):
        if not paired:
            return [[lax.all_gather(chunk, "tp", axis=1, tiled=True)]]
        return [[chunk], [cross(chunk, swap(1))]]

    def opposite_of(chunk):
        return cross(chunk, swap(2)) if paired else None

    def rest_of(opposite, done):
        if not paired:
            return []
        opposite = after(opposite, done)
        return [[opposite], [cross(opposite, swap(1))]]

    offsets = [tp_rank ^ spot for spot in range(4)] if paired else [0]
    pair = tp_rank // 2 * 2
    meta = jnp.stack(
        [tp_rank * units, jnp.int32(units * n_tp), dp_rank, pair * width, (pair ^ 2) * width]
        + [jnp.int32(offset * width) for offset in offsets]
    ).astype(jnp.int32)
    size = unit_block(units, 512)
    flat = lambda blocks: [(piece, "vmem" if spot >= 2 else "whole") for spot, pieces in enumerate(blocks) for piece in pieces]
    counts_of = lambda blocks: tuple(len(pieces) for pieces in blocks)
    kept_outs = [((rows, units), bf16, "cols")] * 2 + [((rows, own), bf16, "whole")] * 2
    partial_outs = [((rows, units), f32, "cols")] * 2
    full = [pltpu.VMEM((rows, model), bf16)] * 2
    half = [pltpu.VMEM((rows, model // 2), bf16)] * 2 if paired else full
    share = lambda columns: 4 * rows * columns * units

    in_hbm = lambda array: pltpu.with_memory_space_constraint(array, pltpu.HBM)
    small = pltpu.CompilerParams(vmem_limit_bytes=LIM * MIB)
    chunk = pl.pallas_call(
        sort_kernel, name="sort_rows", out_shape=jax.ShapeDtypeStruct((2 * rows, width), bf16), compiler_params=small
    )(ordering[None, :], in_hbm(patches), in_hbm(cotangent))

    near = near_of(chunk)
    opposite = opposite_of(chunk)
    coming = onward(chunk)
    if paired:
        weights, *begun = run_kernel(
            functools.partial(open_kernel, counts_of(near)), "open_group", meta, size, units,
            flat(near) + [(w_in, "any"), (w_out, "any")],
            [((2 * model, units), bf16, "vmem")] + partial_outs,
            half + [pltpu.SemaphoreType.DMA((2, units // size))],
            share(model // 2),
            LIM,
        )
        held, done = [(weights, "vmem")], begun[0]
    else:
        held, done, begun = [(w_in, "vmem"), (w_out, "vmem")], meta, []
    chunk = after(coming, done)
    blocks = near + rest_of(opposite, done)
    opposite = opposite_of(chunk)
    coming = onward(chunk)
    *parts, hidden, back_pre, x_cols, c_cols = run_kernel(
        functools.partial(home_kernel, counts_of(blocks), len(held), len(begun)), "home_group", meta, size, units,
        flat(blocks) + held + [(array, "cols") for array in begun],
        [((2 * rows, width if paired else model), bf16, "whole")] * len(blocks) + kept_outs,
        half + [pltpu.VMEM((rows, model), f32)] * 2,
        share(2 * model - model // 2 * len(begun) // 2),
        LIM,
    )
    past = [(hidden, back_pre, x_cols, c_cols)]
    if paired:
        swapped = [cross(parts[1], swap(1)), cross(parts[3], swap(1))]
    for step in range(1, n_dp):
        done = past[-1][0]
        near = near_of(chunk)
        blocks = near + rest_of(opposite, done)
        if step < n_dp - 1:
            chunk = after(coming, done)
            opposite = opposite_of(chunk)
            if step < n_dp - 2:
                coming = onward(chunk)
            past.append(
                run_kernel(
                    functools.partial(away_kernel, counts_of(blocks), len(held)), "away_group", meta, size, units,
                    flat(blocks) + held, kept_outs, full, share(model), LIM,
                )
            )
    begun = []
    if paired:
        begun = run_kernel(
            functools.partial(begin_kernel, counts_of(near), len(held)), "begin_last", meta, size, units,
            flat(near) + held, partial_outs, half, share(model // 2), LIM,
        )
    last_size = unit_block(units, 256)
    everyone = rows * n_dp
    grad_in, grad_out = run_kernel(
        functools.partial(last_kernel, counts_of(blocks), len(held), len(begun), len(past)), "last_group",
        meta, last_size, units,
        flat(blocks) + held + [(array, "cols") for array in begun]
        + [pair for kept in past for pair in zip(kept, ("cols", "cols", "whole", "whole"))],
        [((own, units), f32, "cols"), ((units, own), f32, "rows")],
        half + [
            pltpu.VMEM((rows, own), bf16),
            pltpu.VMEM((own, everyone), bf16),
            pltpu.VMEM((everyone, own), bf16),
            pltpu.VMEM((everyone, last_size), bf16),
            pltpu.VMEM((everyone, last_size), bf16),
        ],
        share(model - model // 2 * len(begun) // 2) + 4 * everyone * own * units,
        LIM,
    )
    if paired:
        far = (after(swapped[1], begun[0]).astype(f32) + parts[2].astype(f32)).astype(bf16)
        sums = [parts[0], swapped[0], cross(far, swap(2))]
    else:
        sums = [lax.psum_scatter(parts[0], "tp", scatter_dimension=1, tiled=True)]
    mixed, grad_patches = pl.pallas_call(
        functools.partial(restore_kernel, len(sums)), name="restore_rows",
        out_shape=[jax.ShapeDtypeStruct((rows, width), bf16)] * 2,
        compiler_params=small,
    )(ordering[None, :], *[in_hbm(after(array, grad_in)) for array in sums])
    return (mixed, grad_patches, grad_in, grad_out)


def solution(mesh):
    return jax.shard_map(
        shards,
        mesh=mesh,
        in_specs=(
            P(("rep", "dp"), "tp"),
            P(("rep", "dp")),
            P(None, "tp"),
            P("tp", None),
            P(("rep", "dp"), "tp"),
        ),
        out_specs=(
            P(("rep", "dp"), "tp"),
            P(("rep", "dp"), "tp"),
            P(("rep", "dp"), "tp"),
            P(("rep", "tp"), "dp"),
        ),
        check_vma=False,
    )
```

```python
import functools
import math

import jax
import jax.numpy as jnp
from jax import lax
from jax.experimental import pallas as pl
from jax.experimental.pallas import tpu as pltpu
from jax.sharding import PartitionSpec as P

LEVELS = 4
MIB = 1024 * 1024
LIM = 23
FIXED = 5
ROOT = math.sqrt(2.0 / math.pi)


def contract_cols(left_side, right_side):
    return lax.dot_general(
        left_side, right_side, (((1,), (1,)), ((), ())), preferred_element_type=jnp.float32
    )


def contract_rows(left_side, right_side):
    return lax.dot_general(
        left_side, right_side, (((0,), (0,)), ((), ())), preferred_element_type=jnp.float32
    )


def gelu_and_slope(pre_act):
    square = pre_act * pre_act
    tanh = jnp.tanh(ROOT * pre_act * (1.0 + 0.044715 * square))
    half = 0.5 * (1.0 + tanh)
    slope = half + 0.5 * pre_act * (1.0 - tanh * tanh) * (ROOT * (1.0 + 0.134145 * square))
    return pre_act * half, slope


def unpack(pieces, at, x_out, c_out, to):
    level = x_out.shape[0] // LEVELS
    first = 0
    for piece in pieces:
        for start in range(0, piece.shape[0], 2 * level):
            x_out[first : first + level, to] = piece[start : start + level, at]
            c_out[first : first + level, to] = piece[start + level : start + 2 * level, at]
            first += level


def fill(meta, blocks, x_full, c_full, base=0, spots=None):
    for spot, pieces in enumerate(blocks):
        if spots is None or spot in spots:
            to = pl.ds(pl.multiple_of(meta[FIXED + spot] - base, 128), pieces[0].shape[1])
            unpack(pieces, slice(None), x_full, c_full, to)


def fill_late(meta, begun, blocks, x_full, c_full):
    if begun:
        fill(meta, blocks, x_full, c_full, meta[4], (2, 3))
    else:
        fill(meta, blocks, x_full, c_full)


def own_columns(meta, blocks, x_cols, c_cols):
    width = x_cols.shape[1]
    start = meta[2] * width
    for spot, pieces in enumerate(blocks):
        wide = pieces[0].shape[1]
        begin = meta[FIXED + spot]

        @pl.when((start >= begin) & (start < begin + wide))
        def _():
            at = pl.ds(pl.multiple_of(start - begin, 128), width) if width < wide else slice(None)
            unpack(pieces, at, x_cols, c_cols, slice(None))


def unit_slice(size, first=0):
    return pl.ds(pl.multiple_of(first + pl.program_id(0) * size, 128), size)


def views(weights):
    if len(weights) == 1:
        half = weights[0].shape[0] // 2
        return weights[0].at[pl.ds(0, half), :], weights[0].at[pl.ds(half, half), :]
    return weights


def products(x_full, c_full, first, weights, units):
    w_first, w_second = weights
    deep = pl.ds(first if isinstance(first, int) else pl.multiple_of(first, 128), x_full.shape[1])
    at = unit_slice(units)
    pre_act = jnp.dot(x_full[...], w_first[deep, at], preferred_element_type=jnp.float32)
    return pre_act, contract_cols(c_full[...], w_second[at, deep])


def activations(meta, pre_act, back_hidden):
    rows, units = pre_act.shape
    hidden, slope = gelu_and_slope(pre_act)
    back_pre = back_hidden * slope
    level = rows // LEVELS
    unit_ids = meta[0] + pl.program_id(0) * units + lax.broadcasted_iota(jnp.int32, (level, units), 1)
    keep = [unit_ids < lax.shift_right_logical(meta[1], level_idx) for level_idx in range(LEVELS)]
    cut = lambda array: jnp.concatenate(
        [
            jnp.where(keep[level_idx], array[level_idx * level : (level_idx + 1) * level], 0.0)
            for level_idx in range(LEVELS)
        ],
        axis=0,
    ).astype(jnp.bfloat16)
    return cut(hidden), cut(back_pre)


def sort_kernel(ordering, patches, cotangent, chunk):
    rows = patches.shape[0]
    level = rows // LEVELS
    patch_ids = lax.broadcasted_iota(jnp.int32, (rows, rows), 0)
    pick = (patch_ids == ordering[...]).astype(jnp.float32).astype(jnp.bfloat16)
    for spot, array in enumerate((patches, cotangent)):
        placed = contract_rows(pick, array[...]).astype(jnp.bfloat16)
        for level_idx in range(LEVELS):
            start = (2 * level_idx + spot) * level
            chunk[start : start + level, :] = placed[level_idx * level : (level_idx + 1) * level]


def restore_kernel(count, ordering, *refs):
    shares, (mixed, grad_patches) = refs[:count], refs[count:]
    rows = mixed.shape[0]
    level = rows // LEVELS
    total = sum(share[...].astype(jnp.float32) for share in shares).astype(jnp.bfloat16)
    patch_ids = lax.broadcasted_iota(jnp.int32, (rows, rows), 0)
    pick = (patch_ids == ordering[...]).astype(jnp.float32).astype(jnp.bfloat16)
    for spot, out in enumerate((mixed, grad_patches)):
        placed = jnp.concatenate(
            [total[(2 * idx + spot) * level : (2 * idx + spot + 1) * level] for idx in range(LEVELS)], axis=0
        )
        out[...] = jnp.dot(pick, placed, preferred_element_type=jnp.float32).astype(jnp.bfloat16)


def split_refs(refs, counts):
    groups = []
    for count in counts:
        groups.append(refs[:count])
        refs = refs[count:]
    return groups, refs


def open_kernel(counts, meta, *refs):
    blocks, (w_in, w_out, weights, pre_out, back_out, x_full, c_full, arrived) = split_refs(refs, counts)
    model, units = w_in.shape[0], pre_out.shape[1]

    def copies(step):
        cols = pl.ds(pl.multiple_of(step * units, 128), units)
        rows = pl.ds(pl.multiple_of(model + step * units, 128), units)
        return (
            pltpu.make_async_copy(w_in.at[:, cols], weights.at[pl.ds(0, model), cols], arrived.at[0, step]),
            pltpu.make_async_copy(w_out.at[cols, :], weights.at[rows, :], arrived.at[1, step]),
        )

    @pl.when(pl.program_id(0) == 0)
    def _():
        for step in range(w_in.shape[1] // units):
            for copy in copies(step):
                copy.start()
        fill(meta, blocks, x_full, c_full, meta[3])

    for copy in copies(pl.program_id(0)):
        copy.wait()
    pre_out[...], back_out[...] = products(x_full, c_full, meta[3], views([weights]), units)


def home_kernel(counts, held, begun, meta, *refs):
    blocks, refs = split_refs(refs, counts)
    (weights, begun, parts), refs = split_refs(refs, (held, begun, len(counts)))
    hidden_out, back_out, x_cols, c_cols, x_full, c_full, total_out, total_in = refs
    step = pl.program_id(0)
    rows, units = hidden_out.shape
    model = total_out.shape[1]
    level = rows // LEVELS

    @pl.when(step == 0)
    def _():
        fill_late(meta, begun, blocks, x_full, c_full)
        own_columns(meta, blocks, x_cols, c_cols)

    hidden, back_pre = late_products(meta, x_full, c_full, begun, weights, units)
    hidden_out[...] = hidden
    back_out[...] = back_pre
    w_first, w_second = views(weights)
    at = unit_slice(units)
    wide = model // 4
    shares = lambda cols: (
        jnp.dot(hidden, w_second[at, cols], preferred_element_type=jnp.float32),
        contract_cols(back_pre, w_first[cols, at]),
    )

    @pl.when(step == 0)
    def _():
        for first in range(0, model, wide):
            cols = pl.ds(first, wide)
            total_out[:, cols], total_in[:, cols] = shares(cols)

    @pl.when(step > 0)
    def _():
        for first in range(0, model, wide):
            cols = pl.ds(first, wide)
            more_out, more_in = shares(cols)
            total_out[:, cols] += more_out
            total_in[:, cols] += more_in

    @pl.when(step == pl.num_programs(0) - 1)
    def _():
        for spot, part in enumerate(parts):
            cols = pl.ds(pl.multiple_of(meta[FIXED + spot], 128), part.shape[1])
            for level_idx in range(LEVELS):
                here = pl.ds(level_idx * level, level)
                start = 2 * level_idx * level
                part[start : start + level, :] = total_out[here, cols].astype(jnp.bfloat16)
                part[start + level : start + 2 * level, :] = total_in[here, cols].astype(jnp.bfloat16)


def late_products(meta, x_full, c_full, begun, weights, units):
    if not begun:
        return activations(meta, *products(x_full, c_full, 0, views(weights), units))
    pre_act, back_hidden = products(x_full, c_full, meta[4], views(weights), units)
    return activations(meta, pre_act + begun[0][...], back_hidden + begun[1][...])


def away_kernel(counts, held, meta, *refs):
    blocks, refs = split_refs(refs, counts)
    weights, (hidden_out, back_out, x_cols, c_cols, x_full, c_full) = refs[:held], refs[held:]

    @pl.when(pl.program_id(0) == 0)
    def _():
        fill(meta, blocks, x_full, c_full)
        own_columns(meta, blocks, x_cols, c_cols)

    hidden_out[...], back_out[...] = late_products(meta, x_full, c_full, (), weights, hidden_out.shape[1])


def last_kernel(counts, held, others, meta, *refs):
    blocks, refs = split_refs(refs, counts)
    (weights, *past), refs = split_refs(refs, (held,) + (4,) * others)
    grad_in, grad_out, x_full, c_full, x_cols, x_turned, c_all, hidden_all, back_all = refs
    rows = x_full.shape[0]
    own = pl.ds(others * rows, rows)

    @pl.when(pl.program_id(0) == 0)
    def _():
        for spot in range(others):
            x_turned[:, pl.ds(spot * rows, rows)] = past[spot][2][...].T
            c_all[pl.ds(spot * rows, rows), :] = past[spot][3][...]
        fill(meta, blocks, x_full, c_full)
        own_columns(meta, blocks, x_cols, c_all.at[own, :])
        x_turned[:, own] = x_cols[...].T

    hidden, back_pre = late_products(meta, x_full, c_full, (), weights, hidden_all.shape[1])
    for spot in range(others):
        hidden_all[pl.ds(spot * rows, rows), :] = past[spot][0][...]
        back_all[pl.ds(spot * rows, rows), :] = past[spot][1][...]
    hidden_all[own, :] = hidden
    back_all[own, :] = back_pre
    grad_in[...] = jnp.dot(x_turned[...], back_all[...], preferred_element_type=jnp.float32)
    grad_out[...] = contract_rows(hidden_all[...], c_all[...])


def unit_block(units, most):
    for size in (1536, 768, 512, 384, 256, 128):
        if size <= most and units % size == 0:
            return size
    return units


def run_kernel(kernel, name, meta, size, units, inputs, outs, scratch, flops, limit):
    def spec(shape, kind):
        zeros = (0,) * len(shape)
        if kind == "whole":
            return pl.BlockSpec(shape, lambda step, meta: zeros, pipeline_mode=pl.Buffered(1))
        if kind == "cols":
            return pl.BlockSpec((shape[0], size), lambda step, meta: (0, step))
        if kind == "rows":
            return pl.BlockSpec((size, shape[1]), lambda step, meta: (step, 0))
        return pl.BlockSpec(memory_space=pltpu.VMEM if kind == "vmem" else pl.ANY)

    resident = lambda array, kind: pltpu.with_memory_space_constraint(array, pltpu.VMEM if kind == "vmem" else pltpu.HBM)
    shape_of = lambda shape, dtype, kind: (
        pltpu.VMEM(shape, dtype) if kind == "vmem" else jax.ShapeDtypeStruct(shape, dtype)
    )
    moved = sum(array.size * array.dtype.itemsize for array, kind in inputs if kind != "vmem")
    moved += sum(math.prod(shape) * jnp.dtype(dtype).itemsize for shape, dtype, kind in outs if kind != "vmem")
    return pl.pallas_call(
        kernel,
        name=name,
        out_shape=[shape_of(*out) for out in outs],
        grid_spec=pltpu.PrefetchScalarGridSpec(
            num_scalar_prefetch=1,
            grid=(units // size,),
            in_specs=[spec(array.shape, kind) for array, kind in inputs],
            out_specs=[spec(shape, kind) for shape, _, kind in outs],
            scratch_shapes=scratch,
        ),
        compiler_params=pltpu.CompilerParams(dimension_semantics=("arbitrary",), vmem_limit_bytes=limit * MIB),
        cost_estimate=pl.CostEstimate(flops=flops // 16, bytes_accessed=moved // 16, transcendentals=0),
    )(meta, *[resident(*pair) for pair in inputs])


def shards(patches, ordering, w_in, w_out, cotangent):
    n_tp, n_dp = lax.axis_size("tp"), lax.axis_size("dp")
    tp_rank, dp_rank = lax.axis_index("tp"), lax.axis_index("dp")
    rows, width = patches.shape
    model, units = w_in.shape
    own = model // n_dp
    bf16, f32 = jnp.bfloat16, jnp.float32
    paired = n_tp == 4 and model == units
    swap = lambda bits: [(rank, rank ^ bits) for rank in range(n_tp)]
    cross = lambda array, pairs: lax.ppermute(array, "tp", pairs)
    onward = lambda array: lax.ppermute(array, "dp", [(rank, (rank + 1) % n_dp) for rank in range(n_dp)])
    back = lambda array: lax.ppermute(array, "dp", [(rank, (rank - 1) % n_dp) for rank in range(n_dp)])
    turned = paired and n_dp > 3
    after = lambda array, done: lax.optimization_barrier((array, done))[0]

    def near_of(chunk):
        if not paired:
            return [[lax.all_gather(chunk, "tp", axis=1, tiled=True)]]
        return [[chunk], [cross(chunk, swap(1))]]

    def opposite_of(chunk):
        return [cross(chunk, swap(2))] if paired else []

    def rest_of(opposite, done):
        if not paired:
            return []
        opposite = [after(piece, done) for piece in opposite]
        return [opposite, [cross(piece, swap(1)) for piece in opposite]]

    offsets = [tp_rank ^ spot for spot in range(4)] if paired else [0]
    pair = tp_rank // 2 * 2
    meta = jnp.stack(
        [tp_rank * units, jnp.int32(units * n_tp), dp_rank, pair * width, (pair ^ 2) * width]
        + [jnp.int32(offset * width) for offset in offsets]
    ).astype(jnp.int32)
    size, away_size = unit_block(units, 512), unit_block(units, 1536)
    flat = lambda blocks: [(piece, "vmem" if spot >= 2 else "whole") for spot, pieces in enumerate(blocks) for piece in pieces]
    counts_of = lambda blocks: tuple(len(pieces) for pieces in blocks)
    kept_outs = [((rows, units), bf16, "cols")] * 2 + [((rows, own), bf16, "whole")] * 2
    partial_outs = [((rows, units), f32, "cols")] * 2
    full = [pltpu.VMEM((rows, model), bf16)] * 2
    half = [pltpu.VMEM((rows, model // 2), bf16)] * 2 if paired else full
    share = lambda columns: 4 * rows * columns * units

    in_hbm = lambda array: pltpu.with_memory_space_constraint(array, pltpu.HBM)
    small = pltpu.CompilerParams(vmem_limit_bytes=LIM * MIB)
    chunk = pl.pallas_call(
        sort_kernel, name="sort_rows", out_shape=jax.ShapeDtypeStruct((2 * rows, width), bf16), compiler_params=small
    )(ordering[None, :], in_hbm(patches), in_hbm(cotangent))

    near = near_of(chunk)
    opposite = opposite_of(chunk)
    own_opposite = opposite[0] if paired else None
    coming = onward(chunk)
    if paired:
        weights, *begun = run_kernel(
            functools.partial(open_kernel, counts_of(near)), "open_group", meta, size, units,
            flat(near) + [(w_in, "any"), (w_out, "any")],
            [((2 * model, units), bf16, "vmem")] + partial_outs,
            half + [pltpu.SemaphoreType.DMA((2, units // size))],
            share(model // 2),
            LIM,
        )
        held, done = [(weights, "vmem")], begun[0]
    else:
        held, done, begun = [(w_in, "vmem"), (w_out, "vmem")], meta, []
    chunk = after(coming, done)
    blocks = near + rest_of(opposite, done)
    opposite = opposite_of(chunk)
    coming = onward(chunk)
    *parts, hidden, back_pre, x_cols, c_cols = run_kernel(
        functools.partial(home_kernel, counts_of(blocks), len(held), len(begun)), "home_group", meta, size, units,
        flat(blocks) + held + [(array, "cols") for array in begun],
        [((2 * rows, width if paired else model), bf16, "whole")] * len(blocks) + kept_outs,
        half + [pltpu.VMEM((rows, model), f32)] * 2,
        share(2 * model - model // 2 * len(begun) // 2),
        LIM,
    )
    past = [(hidden, back_pre, x_cols, c_cols)]
    for step in range(1, n_dp):
        done = past[-1][0]
        near = near_of(chunk)
        blocks = near + rest_of(opposite, done)
        if step < n_dp - 1:
            chunk = after(coming, done)
            if not turned or step < n_dp - 2:
                opposite = opposite_of(chunk)
            else:
                opposite = far_coming
            if turned and step == n_dp - 3:
                coming, far_coming = onward(chunk), [back(after(own_opposite, done))]
            elif step < n_dp - 2:
                coming = onward(chunk)
            past.append(
                run_kernel(
                    functools.partial(away_kernel, counts_of(blocks), len(held)), "away_group", meta, away_size, units,
                    flat(blocks) + held, kept_outs, full, share(model), LIM,
                )
            )
    everyone = rows * n_dp
    grad_in, grad_out = run_kernel(
        functools.partial(last_kernel, counts_of(blocks), len(held), len(past)), "last_group",
        meta, size, units,
        flat(blocks) + held + [pair for kept in past for pair in zip(kept, ("cols", "cols", "whole", "whole"))],
        [((own, units), f32, "cols"), ((units, own), f32, "rows")],
        full + [
            pltpu.VMEM((rows, own), bf16),
            pltpu.VMEM((own, everyone), bf16),
            pltpu.VMEM((everyone, own), bf16),
            pltpu.VMEM((everyone, size), bf16),
            pltpu.VMEM((everyone, size), bf16),
        ],
        share(model) + 4 * everyone * own * units,
        LIM,
    )
    if paired:
        swapped = [cross(after(part, past[-2][0]), swap(1)) for part in parts[1::2]]
        far = (after(swapped[1], past[-1][0]).astype(f32) + parts[2].astype(f32)).astype(bf16)
        sums = [parts[0], swapped[0], cross(far, swap(2))]
    else:
        sums = [lax.psum_scatter(parts[0], "tp", scatter_dimension=1, tiled=True)]
    mixed, grad_patches = pl.pallas_call(
        functools.partial(restore_kernel, len(sums)), name="restore_rows",
        out_shape=[jax.ShapeDtypeStruct((rows, width), bf16)] * 2,
        compiler_params=small,
    )(ordering[None, :], *[after(array, grad_in) for array in sums])
    return (mixed, grad_patches, grad_in, grad_out)


def solution(mesh):
    return jax.shard_map(
        shards,
        mesh=mesh,
        in_specs=(
            P(("rep", "dp"), "tp"),
            P(("rep", "dp")),
            P(None, "tp"),
            P("tp", None),
            P(("rep", "dp"), "tp"),
        ),
        out_specs=(
            P(("rep", "dp"), "tp"),
            P(("rep", "dp"), "tp"),
            P(("rep", "dp"), "tp"),
            P(("rep", "tp"), "dp"),
        ),
        check_vma=False,
    )
```

```python
import functools
import math

import jax
import jax.numpy as jnp
from jax import lax
from jax.experimental import pallas as pl
from jax.experimental.pallas import tpu as pltpu
from jax.sharding import PartitionSpec as P

LEVELS = 4
MIB = 1024 * 1024
LIM = 23
FIXED = 5
ROOT = math.sqrt(2.0 / math.pi)


def contract_cols(left_side, right_side):
    return lax.dot_general(
        left_side, right_side, (((1,), (1,)), ((), ())), preferred_element_type=jnp.float32
    )


def contract_rows(left_side, right_side):
    return lax.dot_general(
        left_side, right_side, (((0,), (0,)), ((), ())), preferred_element_type=jnp.float32
    )


def gelu_and_slope(pre_act):
    square = pre_act * pre_act
    tanh = jnp.tanh(ROOT * pre_act * (1.0 + 0.044715 * square))
    half = 0.5 * (1.0 + tanh)
    slope = half + 0.5 * pre_act * (1.0 - tanh * tanh) * (ROOT * (1.0 + 0.134145 * square))
    return pre_act * half, slope


def unpack(pieces, at, x_out, c_out, to, level, stride, offset=0):
    first = offset
    for piece in pieces:
        for start in range(0, piece.shape[0], 2 * level):
            x_out[first : first + level, to] = piece[start : start + level, at]
            c_out[first : first + level, to] = piece[start + level : start + 2 * level, at]
            first += stride


def fill(meta, blocks, spot, base, x_part, c_part):
    level = x_part.shape[0] // LEVELS
    for more, pieces in enumerate(blocks):
        to = pl.ds(pl.multiple_of(meta[FIXED + spot + more] - base, 128), pieces[0].shape[1])
        unpack(pieces, slice(None), x_part, c_part, to, level, level)


def own_columns(meta, blocks, first_spot, x_cols, c_cols, level, stride, offset=0):
    width = x_cols.shape[1]
    start = meta[2] * width
    for spot, pieces in enumerate(blocks):
        wide = pieces[0].shape[1]
        begin = meta[FIXED + first_spot + spot]

        @pl.when((start >= begin) & (start < begin + wide))
        def _():
            at = pl.ds(pl.multiple_of(start - begin, 128), width) if width < wide else slice(None)
            unpack(pieces, at, x_cols, c_cols, slice(None), level, stride, offset)


def landings(refs, raw, arrived):
    return [pltpu.make_async_copy(ref, raw.at[spot], arrived.at[spot]) for spot, ref in enumerate(refs)]


def level_landings(meta, refs, x_full, c_full, arrived):
    level = x_full.shape[0] // LEVELS
    copies = []
    for spot, ref in enumerate(refs):
        to = pl.ds(pl.multiple_of(meta[FIXED + spot], 128), ref.shape[1])
        for level_idx in range(LEVELS):
            for side, part in enumerate((x_full, c_full)):
                copies.append(
                    pltpu.make_async_copy(
                        ref.at[pl.ds((2 * level_idx + side) * level, level), :],
                        part.at[pl.ds(level_idx * level, level), to],
                        arrived.at[spot, level_idx, side],
                    )
                )
    return copies


def full_columns(meta, x_full, c_full, x_cols, c_cols, level, stride, offset=0):
    width = x_cols.shape[1]
    at = pl.ds(pl.multiple_of(meta[2] * width, 128), width)
    for level_idx in range(LEVELS):
        here, to = pl.ds(level_idx * level, level), pl.ds(offset + level_idx * stride, level)
        x_cols[to, :] = x_full[here, at]
        c_cols[to, :] = c_full[here, at]


def unit_slice(size, first=0):
    return pl.ds(pl.multiple_of(first + pl.program_id(0) * size, 128), size)


def views(weights):
    if len(weights) == 1:
        half = weights[0].shape[0] // 2
        return weights[0].at[pl.ds(0, half), :], weights[0].at[pl.ds(half, half), :]
    return weights


def products(x_full, c_full, first, weights, units):
    w_first, w_second = weights
    deep = pl.ds(first if isinstance(first, int) else pl.multiple_of(first, 128), x_full.shape[1])
    at = unit_slice(units)
    pre_act = jnp.dot(x_full[...], w_first[deep, at], preferred_element_type=jnp.float32)
    return pre_act, contract_cols(c_full[...], w_second[at, deep])


def activations(meta, pre_act, back_hidden):
    rows, units = pre_act.shape
    hidden, slope = gelu_and_slope(pre_act)
    back_pre = back_hidden * slope
    level = rows // LEVELS
    unit_ids = meta[0] + pl.program_id(0) * units + lax.broadcasted_iota(jnp.int32, (level, units), 1)
    keep = [unit_ids < lax.shift_right_logical(meta[1], level_idx) for level_idx in range(LEVELS)]
    cut = lambda array: jnp.concatenate(
        [
            jnp.where(keep[level_idx], array[level_idx * level : (level_idx + 1) * level], 0.0)
            for level_idx in range(LEVELS)
        ],
        axis=0,
    ).astype(jnp.bfloat16)
    return cut(hidden), cut(back_pre)


def sort_kernel(ordering, patches, cotangent, chunk):
    rows = patches.shape[0]
    level = rows // LEVELS
    patch_ids = lax.broadcasted_iota(jnp.int32, (rows, rows), 0)
    pick = (patch_ids == ordering[...]).astype(jnp.float32).astype(jnp.bfloat16)
    for spot, array in enumerate((patches, cotangent)):
        placed = contract_rows(pick, array[...]).astype(jnp.bfloat16)
        for level_idx in range(LEVELS):
            start = (2 * level_idx + spot) * level
            chunk[start : start + level, :] = placed[level_idx * level : (level_idx + 1) * level]


def restore_kernel(count, ordering, *refs):
    shares, (mixed, grad_patches) = refs[:count], refs[count:]
    rows = mixed.shape[0]
    level = rows // LEVELS
    total = sum(share[...].astype(jnp.float32) for share in shares).astype(jnp.bfloat16)
    patch_ids = lax.broadcasted_iota(jnp.int32, (rows, rows), 0)
    pick = (patch_ids == ordering[...]).astype(jnp.float32).astype(jnp.bfloat16)
    for spot, out in enumerate((mixed, grad_patches)):
        placed = jnp.concatenate(
            [total[(2 * idx + spot) * level : (2 * idx + spot + 1) * level] for idx in range(LEVELS)], axis=0
        )
        out[...] = jnp.dot(pick, placed, preferred_element_type=jnp.float32).astype(jnp.bfloat16)


def split_refs(refs, counts):
    groups = []
    for count in counts:
        groups.append(refs[:count])
        refs = refs[count:]
    return groups, refs


def open_kernel(counts, meta, *refs):
    blocks, (w_in, w_out, weights, pre_out, back_out, x_full, c_full, arrived) = split_refs(refs, counts)
    model, units = w_in.shape[0], pre_out.shape[1]

    def copies(step):
        cols = pl.ds(pl.multiple_of(step * units, 128), units)
        rows = pl.ds(pl.multiple_of(model + step * units, 128), units)
        return (
            pltpu.make_async_copy(w_in.at[:, cols], weights.at[pl.ds(0, model), cols], arrived.at[0, step]),
            pltpu.make_async_copy(w_out.at[cols, :], weights.at[rows, :], arrived.at[1, step]),
        )

    @pl.when(pl.program_id(0) == 0)
    def _():
        for step in range(w_in.shape[1] // units):
            for copy in copies(step):
                copy.start()
        fill(meta, blocks, 0, meta[3], x_full, c_full)

    for copy in copies(pl.program_id(0)):
        copy.wait()
    pre_out[...], back_out[...] = products(x_full, c_full, meta[3], views([weights]), units)


def all_products(meta, near, late, x_full, c_full, weights, units, at_near):
    @pl.when(pl.program_id(0) == 0)
    def _():
        for copy in near:
            copy.start()
        fill(meta, late, 2, 0, x_full, c_full)
        for copy in near:
            copy.wait()
        at_near()

    return activations(meta, *products(x_full, c_full, 0, weights, units))


def home_kernel(near_count, counts, held, begun, meta, *refs):
    near, refs = refs[:near_count], refs[near_count:]
    late, refs = split_refs(refs, counts)
    (weights, begun, parts), refs = split_refs(refs, (held, begun, near_count + len(counts)))
    hidden_out, back_out, x_cols, c_cols, raw, arrived, x_part, c_part, total_out, total_in = refs
    blocks = [[raw.at[spot]] for spot in range(near_count)]
    near = landings(near, raw, arrived)
    step = pl.program_id(0)
    rows, units = hidden_out.shape
    model = total_out.shape[1]
    level = rows // LEVELS
    weights = views(weights)

    @pl.when(step == 0)
    def _():
        for copy in near:
            copy.start()
        if begun:
            fill(meta, late, 2, meta[4], x_part, c_part)
        else:
            for copy in near:
                copy.wait()
            fill(meta, blocks, 0, meta[3], x_part, c_part)

    pre_act, back_hidden = products(x_part, c_part, meta[4] if begun else meta[3], weights, units)
    if begun:
        pre_act, back_hidden = pre_act + begun[0][...], back_hidden + begun[1][...]
    hidden, back_pre = activations(meta, pre_act, back_hidden)
    hidden_out[...] = hidden
    back_out[...] = back_pre
    w_first, w_second = weights
    at = unit_slice(units)
    wide = model // 4
    shares = lambda cols: (
        jnp.dot(hidden, w_second[at, cols], preferred_element_type=jnp.float32),
        contract_cols(back_pre, w_first[cols, at]),
    )

    @pl.when(step == 0)
    def _():
        for first in range(0, model, wide):
            cols = pl.ds(first, wide)
            total_out[:, cols], total_in[:, cols] = shares(cols)

    @pl.when(step > 0)
    def _():
        for first in range(0, model, wide):
            cols = pl.ds(first, wide)
            more_out, more_in = shares(cols)
            total_out[:, cols] += more_out
            total_in[:, cols] += more_in

    @pl.when(step == pl.num_programs(0) - 1)
    def _():
        if begun:
            for copy in near:
                copy.wait()
        own_columns(meta, blocks + late, 0, x_cols, c_cols, level, level)
        for spot, part in enumerate(parts):
            cols = pl.ds(pl.multiple_of(meta[FIXED + spot], 128), part.shape[1])
            for level_idx in range(LEVELS):
                here = pl.ds(level_idx * level, level)
                start = 2 * level_idx * level
                part[start : start + level, :] = total_out[here, cols].astype(jnp.bfloat16)
                part[start + level : start + 2 * level, :] = total_in[here, cols].astype(jnp.bfloat16)


def away_kernel(near_count, counts, held, meta, *refs):
    near, refs = refs[:near_count], refs[near_count:]
    late, refs = split_refs(refs, counts)
    weights, (hidden_out, back_out, x_cols, c_cols, arrived, x_full, c_full) = refs[:held], refs[held:]
    near = level_landings(meta, near, x_full, c_full, arrived)
    level = hidden_out.shape[0] // LEVELS
    hidden_out[...], back_out[...] = all_products(
        meta, near, late, x_full, c_full, views(weights), hidden_out.shape[1],
        lambda: full_columns(meta, x_full, c_full, x_cols, c_cols, level, level),
    )


def last_kernel(near_count, counts, held, others, meta, *refs):
    near, refs = refs[:near_count], refs[near_count:]
    late, refs = split_refs(refs, counts)
    (weights, *past), refs = split_refs(refs, (held,) + (4,) * others)
    grad_in, grad_out, x_full, c_full, x_cols, c_all, x_turned, hidden_all, back_all = refs
    rows = x_full.shape[0]
    level = rows // LEVELS
    own = pl.ds(others * rows, rows)

    @pl.when(pl.program_id(0) == 0)
    def _():
        for spot in range(others):
            x_turned[:, pl.ds(spot * rows, rows)] = past[spot][2][...].T
            c_all[pl.ds(spot * rows, rows), :] = past[spot][3][...]
        fill(meta, [[ref] for ref in near], 0, 0, x_full, c_full)
        fill(meta, late, 2, 0, x_full, c_full)
        full_columns(meta, x_full, c_full, x_cols, c_all.at[own, :], level, level)
        x_turned[:, own] = x_cols[...].T

    hidden, back_pre = activations(
        meta, *products(x_full, c_full, 0, views(weights), hidden_all.shape[1])
    )
    for spot in range(others):
        hidden_all[pl.ds(spot * rows, rows), :] = past[spot][0][...]
        back_all[pl.ds(spot * rows, rows), :] = past[spot][1][...]
    hidden_all[own, :] = hidden
    back_all[own, :] = back_pre
    grad_in[...] = jnp.dot(x_turned[...], back_all[...], preferred_element_type=jnp.float32)
    grad_out[...] = contract_rows(hidden_all[...], c_all[...])


def unit_block(units, most):
    for size in (1536, 768, 512, 384, 256, 128):
        if size <= most and units % size == 0:
            return size
    return units


def run_kernel(kernel, name, meta, size, units, inputs, outs, scratch, flops, limit):
    def spec(shape, kind):
        zeros = (0,) * len(shape)
        if kind == "whole":
            return pl.BlockSpec(shape, lambda step, meta: zeros, pipeline_mode=pl.Buffered(1))
        if kind == "cols":
            return pl.BlockSpec((shape[0], size), lambda step, meta: (0, step))
        if kind == "rows":
            return pl.BlockSpec((size, shape[1]), lambda step, meta: (step, 0))
        return pl.BlockSpec(memory_space=pltpu.VMEM if kind == "vmem" else pl.ANY)

    resident = lambda array, kind: pltpu.with_memory_space_constraint(array, pltpu.VMEM if kind == "vmem" else pltpu.HBM)
    shape_of = lambda shape, dtype, kind: (
        pltpu.VMEM(shape, dtype) if kind == "vmem" else jax.ShapeDtypeStruct(shape, dtype)
    )
    moved = sum(array.size * array.dtype.itemsize for array, kind in inputs if kind != "vmem")
    moved += sum(math.prod(shape) * jnp.dtype(dtype).itemsize for shape, dtype, kind in outs if kind != "vmem")
    return pl.pallas_call(
        kernel,
        name=name,
        out_shape=[shape_of(*out) for out in outs],
        grid_spec=pltpu.PrefetchScalarGridSpec(
            num_scalar_prefetch=1,
            grid=(units // size,),
            in_specs=[spec(array.shape, kind) for array, kind in inputs],
            out_specs=[spec(shape, kind) for shape, _, kind in outs],
            scratch_shapes=scratch,
        ),
        compiler_params=pltpu.CompilerParams(dimension_semantics=("arbitrary",), vmem_limit_bytes=limit * MIB),
        cost_estimate=pl.CostEstimate(flops=flops // 16, bytes_accessed=moved // 16, transcendentals=0),
    )(meta, *[resident(*pair) for pair in inputs])


def shards(patches, ordering, w_in, w_out, cotangent):
    n_tp, n_dp = lax.axis_size("tp"), lax.axis_size("dp")
    tp_rank, dp_rank = lax.axis_index("tp"), lax.axis_index("dp")
    rows, width = patches.shape
    model, units = w_in.shape
    own = model // n_dp
    bf16, f32 = jnp.bfloat16, jnp.float32
    paired = n_tp == 4 and model == units
    swap = lambda bits: [(rank, rank ^ bits) for rank in range(n_tp)]
    cross = lambda array, pairs: lax.ppermute(array, "tp", pairs)
    onward = lambda array: lax.ppermute(array, "dp", [(rank, (rank + 1) % n_dp) for rank in range(n_dp)])
    back = lambda array: lax.ppermute(array, "dp", [(rank, (rank - 1) % n_dp) for rank in range(n_dp)])
    turned = paired and n_dp > 3
    after = lambda array, done: lax.optimization_barrier((array, done))[0]

    def near_of(chunk):
        if not paired:
            return [[lax.all_gather(chunk, "tp", axis=1, tiled=True)]]
        return [[chunk], [cross(chunk, swap(1))]]

    def opposite_of(chunk):
        return [cross(chunk, swap(2))] if paired else []

    def rest_of(opposite, done):
        if not paired:
            return []
        opposite = [after(piece, done) for piece in opposite]
        return [opposite, [cross(piece, swap(1)) for piece in opposite]]

    offsets = [tp_rank ^ spot for spot in range(4)] if paired else [0]
    pair = tp_rank // 2 * 2 if paired else 0
    meta = jnp.stack(
        [tp_rank * units, jnp.int32(units * n_tp), dp_rank, jnp.int32(pair * width), jnp.int32((pair ^ 2) * width)]
        + [jnp.int32(offset * width) for offset in offsets]
    ).astype(jnp.int32)
    size, away_size = unit_block(units, 512), unit_block(units, 1536)
    flat = lambda blocks, kind: [(piece, kind) for pieces in blocks for piece in pieces]
    counts_of = lambda blocks: tuple(len(pieces) for pieces in blocks)
    kept_outs = [((rows, units), bf16, "cols")] * 2 + [((rows, own), bf16, "whole")] * 2
    partial_outs = [((rows, units), f32, "cols")] * 2
    full = [pltpu.VMEM((rows, model), bf16)] * 2
    half = [pltpu.VMEM((rows, model // 2 if paired else model), bf16)] * 2
    n_near = 2 if paired else 1
    level_landing = [pltpu.SemaphoreType.DMA((n_near, LEVELS, 2))]
    landing = [pltpu.VMEM((n_near, 2 * rows, width if paired else model), bf16), pltpu.SemaphoreType.DMA((n_near,))]
    share = lambda columns: 4 * rows * columns * units

    in_hbm = lambda array: pltpu.with_memory_space_constraint(array, pltpu.HBM)
    small = pltpu.CompilerParams(vmem_limit_bytes=LIM * MIB)
    chunk = pl.pallas_call(
        sort_kernel, name="sort_rows", out_shape=jax.ShapeDtypeStruct((2 * rows, width), bf16), compiler_params=small
    )(in_hbm(ordering[None, :]), in_hbm(patches), in_hbm(cotangent))

    near = near_of(chunk)
    opposite = opposite_of(chunk)
    own_opposite = opposite[0] if paired else None
    coming = onward(chunk)
    if paired:
        weights, *begun = run_kernel(
            functools.partial(open_kernel, counts_of(near)), "open_group", meta, size, units,
            flat(near, "whole") + [(w_in, "any"), (w_out, "any")],
            [((2 * model, units), bf16, "vmem")] + partial_outs,
            half + [pltpu.SemaphoreType.DMA((2, units // size))],
            share(model // 2),
            LIM,
        )
        held, done = [(weights, "vmem")], begun[0]
    else:
        held, done, begun = [(w_in, "vmem"), (w_out, "vmem")], meta, []
    chunk = after(coming, done)
    late = rest_of(opposite, done)
    opposite = opposite_of(chunk)
    coming = onward(chunk)
    *parts, hidden, back_pre, x_cols, c_cols = run_kernel(
        functools.partial(home_kernel, n_near, counts_of(late), len(held), len(begun)), "home_group", meta, size, units,
        flat(near, "any") + flat(late, "vmem") + held + [(array, "cols") for array in begun],
        [((2 * rows, width if paired else model), bf16, "whole")] * len(offsets) + kept_outs,
        landing + half + [pltpu.VMEM((rows, model), f32)] * 2,
        share(2 * model - model // 2 * len(begun) // 2),
        LIM,
    )
    past = [(hidden, back_pre, x_cols, c_cols)]
    for step in range(1, n_dp):
        done = past[-1][0]
        near = near_of(chunk)
        late = rest_of(opposite, done)
        if step < n_dp - 1:
            chunk = after(coming, done)
            if not turned or step < n_dp - 2:
                opposite = opposite_of(chunk)
            else:
                opposite = far_coming
            if turned and step == n_dp - 3:
                coming = onward(chunk)
                far_coming = [back(after(own_opposite, done))]
            elif step < n_dp - 2:
                coming = onward(chunk)
            past.append(
                run_kernel(
                    functools.partial(away_kernel, n_near, counts_of(late), len(held)), "away_group",
                    meta, away_size, units, flat(near, "any") + flat(late, "vmem") + held, kept_outs,
                    level_landing + full, share(model), LIM,
                )
            )
    everyone = rows * n_dp
    grad_in, grad_out = run_kernel(
        functools.partial(last_kernel, n_near, counts_of(late), len(held), len(past)), "last_group", meta, size, units,
        flat(near, "whole") + flat(late, "vmem") + held
        + [pair for kept in past for pair in zip(kept, ("cols", "cols", "whole", "whole"))],
        [((own, units), f32, "cols"), ((units, own), f32, "rows")],
        full + [
            pltpu.VMEM((rows, own), bf16),
            pltpu.VMEM((everyone, own), bf16),
            pltpu.VMEM((own, everyone), bf16),
            pltpu.VMEM((everyone, size), bf16),
            pltpu.VMEM((everyone, size), bf16),
        ],
        share(model) + 4 * everyone * own * units,
        LIM,
    )
    if paired:
        swapped = [cross(after(part, past[-2][0]), swap(1)) for part in parts[1::2]]
        far = (after(swapped[1], past[-1][0]).astype(f32) + parts[2].astype(f32)).astype(bf16)
        sums = [parts[0], swapped[0], cross(far, swap(2))]
    else:
        sums = [lax.psum_scatter(parts[0], "tp", scatter_dimension=1, tiled=True)]
    mixed, grad_patches = pl.pallas_call(
        functools.partial(restore_kernel, len(sums)), name="restore_rows",
        out_shape=[jax.ShapeDtypeStruct((rows, width), bf16)] * 2,
        compiler_params=small,
    )(ordering[None, :], *[after(array, grad_in) for array in sums])
    return (mixed, grad_patches, grad_in, grad_out)


def solution(mesh):
    return jax.shard_map(
        shards,
        mesh=mesh,
        in_specs=(
            P(("rep", "dp"), "tp"),
            P(("rep", "dp")),
            P(None, "tp"),
            P("tp", None),
            P(("rep", "dp"), "tp"),
        ),
        out_specs=(
            P(("rep", "dp"), "tp"),
            P(("rep", "dp"), "tp"),
            P(("rep", "dp"), "tp"),
            P(("rep", "tp"), "dp"),
        ),
        check_vma=False,
    )
```

```python
import functools
import math

import jax
import jax.numpy as jnp
from jax import lax
from jax.experimental import pallas as pl
from jax.experimental.pallas import tpu as pltpu
from jax.sharding import PartitionSpec as P

LEVELS = 4
MIB = 1024 * 1024
LIM = 23
FIXED = 5
ROOT = math.sqrt(2.0 / math.pi)


def contract_cols(left_side, right_side):
    return lax.dot_general(
        left_side, right_side, (((1,), (1,)), ((), ())), preferred_element_type=jnp.float32
    )


def contract_rows(left_side, right_side):
    return lax.dot_general(
        left_side, right_side, (((0,), (0,)), ((), ())), preferred_element_type=jnp.float32
    )


def gelu_and_slope(pre_act):
    square = pre_act * pre_act
    tanh = jnp.tanh(ROOT * pre_act * (1.0 + 0.044715 * square))
    half = 0.5 * (1.0 + tanh)
    slope = half + 0.5 * pre_act * (1.0 - tanh * tanh) * (ROOT * (1.0 + 0.134145 * square))
    return pre_act * half, slope


def unpack(pieces, at, x_out, c_out, to, level, stride, offset=0):
    first = offset
    for piece in pieces:
        for start in range(0, piece.shape[0], 2 * level):
            x_out[first : first + level, to] = piece[start : start + level, at]
            c_out[first : first + level, to] = piece[start + level : start + 2 * level, at]
            first += stride


def fill(meta, blocks, spot, base, x_part, c_part):
    level = x_part.shape[0] // LEVELS
    for more, pieces in enumerate(blocks):
        to = pl.ds(pl.multiple_of(meta[FIXED + spot + more] - base, 128), pieces[0].shape[1])
        unpack(pieces, slice(None), x_part, c_part, to, level, level)


def own_columns(meta, blocks, first_spot, x_cols, c_cols, level, stride, offset=0):
    width = x_cols.shape[1]
    start = meta[2] * width
    for spot, pieces in enumerate(blocks):
        wide = pieces[0].shape[1]
        begin = meta[FIXED + first_spot + spot]

        @pl.when((start >= begin) & (start < begin + wide))
        def _():
            at = pl.ds(pl.multiple_of(start - begin, 128), width) if width < wide else slice(None)
            unpack(pieces, at, x_cols, c_cols, slice(None), level, stride, offset)


def landings(refs, raw, arrived):
    return [pltpu.make_async_copy(ref, raw.at[spot], arrived.at[spot]) for spot, ref in enumerate(refs)]


def level_landings(meta, refs, x_full, c_full, arrived):
    level = x_full.shape[0] // LEVELS
    copies = []
    for spot, ref in enumerate(refs):
        to = pl.ds(pl.multiple_of(meta[FIXED + spot], 128), ref.shape[1])
        for level_idx in range(LEVELS):
            for side, part in enumerate((x_full, c_full)):
                copies.append(
                    pltpu.make_async_copy(
                        ref.at[pl.ds((2 * level_idx + side) * level, level), :],
                        part.at[pl.ds(level_idx * level, level), to],
                        arrived.at[spot, level_idx, side],
                    )
                )
    return copies


def full_columns(meta, x_full, c_full, x_cols, c_cols, level, stride, offset=0):
    width = x_cols.shape[1]
    at = pl.ds(pl.multiple_of(meta[2] * width, 128), width)
    for level_idx in range(LEVELS):
        here, to = pl.ds(level_idx * level, level), pl.ds(offset + level_idx * stride, level)
        x_cols[to, :] = x_full[here, at]
        c_cols[to, :] = c_full[here, at]


def unit_slice(size, first=0):
    return pl.ds(pl.multiple_of(first + pl.program_id(0) * size, 128), size)


def views(weights):
    if len(weights) == 1:
        half = weights[0].shape[0] // 2
        return weights[0].at[pl.ds(0, half), :], weights[0].at[pl.ds(half, half), :]
    return weights


def products(x_full, c_full, first, weights, units):
    w_first, w_second = weights
    deep = pl.ds(first if isinstance(first, int) else pl.multiple_of(first, 128), x_full.shape[1])
    at = unit_slice(units)
    pre_act = jnp.dot(x_full[...], w_first[deep, at], preferred_element_type=jnp.float32)
    return pre_act, contract_cols(c_full[...], w_second[at, deep])


def activations(meta, pre_act, back_hidden):
    rows, units = pre_act.shape
    hidden, slope = gelu_and_slope(pre_act)
    back_pre = back_hidden * slope
    level = rows // LEVELS
    unit_ids = meta[0] + pl.program_id(0) * units + lax.broadcasted_iota(jnp.int32, (level, units), 1)
    keep = [unit_ids < lax.shift_right_logical(meta[1], level_idx) for level_idx in range(LEVELS)]
    cut = lambda array: jnp.concatenate(
        [
            jnp.where(keep[level_idx], array[level_idx * level : (level_idx + 1) * level], 0.0)
            for level_idx in range(LEVELS)
        ],
        axis=0,
    ).astype(jnp.bfloat16)
    return cut(hidden), cut(back_pre)


def sort_kernel(ordering, patches, cotangent, chunk):
    rows = patches.shape[0]
    level = rows // LEVELS
    patch_ids = lax.broadcasted_iota(jnp.int32, (rows, rows), 0)
    pick = (patch_ids == ordering[...]).astype(jnp.float32).astype(jnp.bfloat16)
    for spot, array in enumerate((patches, cotangent)):
        placed = contract_rows(pick, array[...]).astype(jnp.bfloat16)
        for level_idx in range(LEVELS):
            start = (2 * level_idx + spot) * level
            chunk[start : start + level, :] = placed[level_idx * level : (level_idx + 1) * level]


def restore_kernel(count, ordering, *refs):
    shares, (mixed, grad_patches) = refs[:count], refs[count:]
    rows = mixed.shape[0]
    level = rows // LEVELS
    total = sum(share[...].astype(jnp.float32) for share in shares).astype(jnp.bfloat16)
    patch_ids = lax.broadcasted_iota(jnp.int32, (rows, rows), 0)
    pick = (patch_ids == ordering[...]).astype(jnp.float32).astype(jnp.bfloat16)
    for spot, out in enumerate((mixed, grad_patches)):
        placed = jnp.concatenate(
            [total[(2 * idx + spot) * level : (2 * idx + spot + 1) * level] for idx in range(LEVELS)], axis=0
        )
        out[...] = jnp.dot(pick, placed, preferred_element_type=jnp.float32).astype(jnp.bfloat16)


def split_refs(refs, counts):
    groups = []
    for count in counts:
        groups.append(refs[:count])
        refs = refs[count:]
    return groups, refs


def open_kernel(counts, meta, *refs):
    blocks, (w_in, w_out, weights, pre_out, back_out, x_full, c_full, arrived) = split_refs(refs, counts)
    model, units = w_in.shape[0], pre_out.shape[1]

    def copies(step):
        cols = pl.ds(pl.multiple_of(step * units, 128), units)
        rows = pl.ds(pl.multiple_of(model + step * units, 128), units)
        return (
            pltpu.make_async_copy(w_in.at[:, cols], weights.at[pl.ds(0, model), cols], arrived.at[0, step]),
            pltpu.make_async_copy(w_out.at[cols, :], weights.at[rows, :], arrived.at[1, step]),
        )

    @pl.when(pl.program_id(0) == 0)
    def _():
        for step in range(w_in.shape[1] // units):
            for copy in copies(step):
                copy.start()
        fill(meta, blocks, 0, meta[3], x_full, c_full)

    for copy in copies(pl.program_id(0)):
        copy.wait()
    pre_out[...], back_out[...] = products(x_full, c_full, meta[3], views([weights]), units)


def all_products(meta, near, late, x_full, c_full, weights, units, at_near):
    @pl.when(pl.program_id(0) == 0)
    def _():
        for copy in near:
            copy.start()
        fill(meta, late, 2, 0, x_full, c_full)
        for copy in near:
            copy.wait()
        at_near()

    return activations(meta, *products(x_full, c_full, 0, weights, units))


def home_kernel(near_count, counts, held, begun, meta, *refs):
    near, refs = refs[:near_count], refs[near_count:]
    late, refs = split_refs(refs, counts)
    (weights, begun, parts), refs = split_refs(refs, (held, begun, near_count + len(counts)))
    hidden_out, back_out, x_cols, c_cols, raw, arrived, x_part, c_part, total_out, total_in = refs
    blocks = [[raw.at[spot]] for spot in range(near_count)]
    near = landings(near, raw, arrived)
    step = pl.program_id(0)
    rows, units = hidden_out.shape
    model = total_out.shape[1]
    level = rows // LEVELS
    weights = views(weights)

    @pl.when(step == 0)
    def _():
        for copy in near:
            copy.start()
        if begun:
            fill(meta, late, 2, meta[4], x_part, c_part)
        else:
            for copy in near:
                copy.wait()
            fill(meta, blocks, 0, meta[3], x_part, c_part)

    pre_act, back_hidden = products(x_part, c_part, meta[4] if begun else meta[3], weights, units)
    if begun:
        pre_act, back_hidden = pre_act + begun[0][...], back_hidden + begun[1][...]
    hidden, back_pre = activations(meta, pre_act, back_hidden)
    hidden_out[...] = hidden
    back_out[...] = back_pre
    w_first, w_second = weights
    at = unit_slice(units)
    wide = model // 4
    shares = lambda cols: (
        jnp.dot(hidden, w_second[at, cols], preferred_element_type=jnp.float32),
        contract_cols(back_pre, w_first[cols, at]),
    )

    @pl.when(step == 0)
    def _():
        for first in range(0, model, wide):
            cols = pl.ds(first, wide)
            total_out[:, cols], total_in[:, cols] = shares(cols)

    @pl.when(step > 0)
    def _():
        for first in range(0, model, wide):
            cols = pl.ds(first, wide)
            more_out, more_in = shares(cols)
            total_out[:, cols] += more_out
            total_in[:, cols] += more_in

    @pl.when(step == pl.num_programs(0) - 1)
    def _():
        if begun:
            for copy in near:
                copy.wait()
        own_columns(meta, blocks + late, 0, x_cols, c_cols, level, level)
        for spot, part in enumerate(parts):
            cols = pl.ds(pl.multiple_of(meta[FIXED + spot], 128), part.shape[1])
            for level_idx in range(LEVELS):
                here = pl.ds(level_idx * level, level)
                start = 2 * level_idx * level
                part[start : start + level, :] = total_out[here, cols].astype(jnp.bfloat16)
                part[start + level : start + 2 * level, :] = total_in[here, cols].astype(jnp.bfloat16)


def away_kernel(near_count, counts, held, meta, *refs):
    near, refs = refs[:near_count], refs[near_count:]
    late, refs = split_refs(refs, counts)
    weights, (hidden_out, back_out, x_cols, c_cols, arrived, x_full, c_full) = refs[:held], refs[held:]
    near = level_landings(meta, near, x_full, c_full, arrived)
    level = hidden_out.shape[0] // LEVELS
    hidden_out[...], back_out[...] = all_products(
        meta, near, late, x_full, c_full, views(weights), hidden_out.shape[1],
        lambda: full_columns(meta, x_full, c_full, x_cols, c_cols, level, level),
    )


def last_kernel(near_count, counts, held, others, meta, *refs):
    near, refs = refs[:near_count], refs[near_count:]
    late, refs = split_refs(refs, counts)
    (weights, *past), refs = split_refs(refs, (held,) + (4,) * others)
    grad_in, grad_out, x_full, c_full, x_cols, c_all, x_turned, hidden_all, back_all = refs
    rows = x_full.shape[0]
    level = rows // LEVELS
    own = pl.ds(others * rows, rows)

    @pl.when(pl.program_id(0) == 0)
    def _():
        for spot in range(others):
            x_turned[:, pl.ds(spot * rows, rows)] = past[spot][2][...].T
            c_all[pl.ds(spot * rows, rows), :] = past[spot][3][...]
        fill(meta, [[ref] for ref in near], 0, 0, x_full, c_full)
        fill(meta, late, 2, 0, x_full, c_full)
        full_columns(meta, x_full, c_full, x_cols, c_all.at[own, :], level, level)
        x_turned[:, own] = x_cols[...].T

    hidden, back_pre = activations(
        meta, *products(x_full, c_full, 0, views(weights), hidden_all.shape[1])
    )
    for spot in range(others):
        hidden_all[pl.ds(spot * rows, rows), :] = past[spot][0][...]
        back_all[pl.ds(spot * rows, rows), :] = past[spot][1][...]
    hidden_all[own, :] = hidden
    back_all[own, :] = back_pre
    grad_in[...] = jnp.dot(x_turned[...], back_all[...], preferred_element_type=jnp.float32)
    grad_out[...] = contract_rows(hidden_all[...], c_all[...])


def unit_block(units, most):
    for size in (1536, 768, 512, 384, 256, 128):
        if size <= most and units % size == 0:
            return size
    return units


def run_kernel(kernel, name, meta, size, units, inputs, outs, scratch, flops, limit):
    def spec(shape, kind):
        zeros = (0,) * len(shape)
        if kind == "whole":
            return pl.BlockSpec(shape, lambda step, meta: zeros, pipeline_mode=pl.Buffered(1))
        if kind == "cols":
            return pl.BlockSpec((shape[0], size), lambda step, meta: (0, step))
        if kind == "rows":
            return pl.BlockSpec((size, shape[1]), lambda step, meta: (step, 0))
        return pl.BlockSpec(memory_space=pltpu.VMEM if kind == "vmem" else pl.ANY)

    resident = lambda array, kind: pltpu.with_memory_space_constraint(array, pltpu.VMEM if kind == "vmem" else pltpu.HBM)
    shape_of = lambda shape, dtype, kind: (
        pltpu.VMEM(shape, dtype) if kind == "vmem" else jax.ShapeDtypeStruct(shape, dtype)
    )
    moved = sum(array.size * array.dtype.itemsize for array, kind in inputs if kind != "vmem")
    moved += sum(math.prod(shape) * jnp.dtype(dtype).itemsize for shape, dtype, kind in outs if kind != "vmem")
    return pl.pallas_call(
        kernel,
        name=name,
        out_shape=[shape_of(*out) for out in outs],
        grid_spec=pltpu.PrefetchScalarGridSpec(
            num_scalar_prefetch=1,
            grid=(units // size,),
            in_specs=[spec(array.shape, kind) for array, kind in inputs],
            out_specs=[spec(shape, kind) for shape, _, kind in outs],
            scratch_shapes=scratch,
        ),
        compiler_params=pltpu.CompilerParams(dimension_semantics=("arbitrary",), vmem_limit_bytes=limit * MIB),
        cost_estimate=pl.CostEstimate(flops=flops // 16, bytes_accessed=moved // 16, transcendentals=0),
    )(meta, *[resident(*pair) for pair in inputs])


def shards(patches, ordering, w_in, w_out, cotangent):
    n_tp, n_dp = lax.axis_size("tp"), lax.axis_size("dp")
    tp_rank, dp_rank = lax.axis_index("tp"), lax.axis_index("dp")
    rows, width = patches.shape
    model, units = w_in.shape
    own = model // n_dp
    bf16, f32 = jnp.bfloat16, jnp.float32
    paired = n_tp == 4 and model == units
    swap = lambda bits: [(rank, rank ^ bits) for rank in range(n_tp)]
    cross = lambda array, pairs: lax.ppermute(array, "tp", pairs)
    onward = lambda array: lax.ppermute(array, "dp", [(rank, (rank + 1) % n_dp) for rank in range(n_dp)])
    back = lambda array: lax.ppermute(array, "dp", [(rank, (rank - 1) % n_dp) for rank in range(n_dp)])
    turned = paired and n_dp > 3
    after = lambda array, done: lax.optimization_barrier((array, done))[0]

    def near_of(chunk):
        if not paired:
            return [[lax.all_gather(chunk, "tp", axis=1, tiled=True)]]
        return [[chunk], [cross(chunk, swap(1))]]

    def opposite_of(chunk):
        return [cross(chunk, swap(2))] if paired else []

    def rest_of(opposite, done):
        if not paired:
            return []
        opposite = [after(piece, done) for piece in opposite]
        return [opposite, [cross(piece, swap(1)) for piece in opposite]]

    offsets = [tp_rank ^ spot for spot in range(4)] if paired else [0]
    pair = tp_rank // 2 * 2 if paired else 0
    meta = jnp.stack(
        [tp_rank * units, jnp.int32(units * n_tp), dp_rank, jnp.int32(pair * width), jnp.int32((pair ^ 2) * width)]
        + [jnp.int32(offset * width) for offset in offsets]
    ).astype(jnp.int32)
    size, home_size, away_size = unit_block(units, 512), unit_block(units, 768), unit_block(units, 1536)
    flat = lambda blocks, kind: [(piece, kind) for pieces in blocks for piece in pieces]
    counts_of = lambda blocks: tuple(len(pieces) for pieces in blocks)
    kept_outs = [((rows, units), bf16, "cols")] * 2 + [((rows, own), bf16, "whole")] * 2
    partial_outs = [((rows, units), f32, "cols")] * 2
    full = [pltpu.VMEM((rows, model), bf16)] * 2
    half = [pltpu.VMEM((rows, model // 2 if paired else model), bf16)] * 2
    n_near = 2 if paired else 1
    level_landing = [pltpu.SemaphoreType.DMA((n_near, LEVELS, 2))]
    landing = [pltpu.VMEM((n_near, 2 * rows, width if paired else model), bf16), pltpu.SemaphoreType.DMA((n_near,))]
    share = lambda columns: 4 * rows * columns * units

    in_hbm = lambda array: pltpu.with_memory_space_constraint(array, pltpu.HBM)
    small = pltpu.CompilerParams(vmem_limit_bytes=LIM * MIB)
    chunk = pl.pallas_call(
        sort_kernel, name="sort_rows", out_shape=jax.ShapeDtypeStruct((2 * rows, width), bf16), compiler_params=small
    )(in_hbm(ordering[None, :]), in_hbm(patches), in_hbm(cotangent))

    near = near_of(chunk)
    opposite = opposite_of(chunk)
    own_opposite = opposite[0] if paired else None
    coming = onward(chunk)
    if paired:
        weights, *begun = run_kernel(
            functools.partial(open_kernel, counts_of(near)), "open_group", meta, size, units,
            flat(near, "whole") + [(w_in, "any"), (w_out, "any")],
            [((2 * model, units), bf16, "vmem")] + partial_outs,
            half + [pltpu.SemaphoreType.DMA((2, units // size))],
            share(model // 2),
            LIM,
        )
        held, done = [(weights, "vmem")], begun[0]
    else:
        held, done, begun = [(w_in, "vmem"), (w_out, "vmem")], meta, []
    chunk = after(coming, done)
    late = rest_of(opposite, done)
    opposite = opposite_of(chunk)
    coming = onward(chunk)
    *parts, hidden, back_pre, x_cols, c_cols = run_kernel(
        functools.partial(home_kernel, n_near, counts_of(late), len(held), len(begun)), "home_group", meta, home_size, units,
        flat(near, "any") + flat(late, "vmem") + held + [(array, "cols") for array in begun],
        [((2 * rows, width if paired else model), bf16, "whole")] * len(offsets) + kept_outs,
        landing + half + [pltpu.VMEM((rows, model), f32)] * 2,
        share(2 * model - model // 2 * len(begun) // 2),
        LIM,
    )
    past = [(hidden, back_pre, x_cols, c_cols)]
    for step in range(1, n_dp):
        done = past[-1][0]
        near = near_of(chunk)
        late = rest_of(opposite, done)
        if step < n_dp - 1:
            chunk = after(coming, done)
            if not turned or step < n_dp - 2:
                opposite = opposite_of(chunk)
            else:
                opposite = far_coming
            if turned and step == n_dp - 3:
                coming = onward(chunk)
                far_coming = [back(after(own_opposite, done))]
            elif step < n_dp - 2:
                coming = onward(chunk)
            past.append(
                run_kernel(
                    functools.partial(away_kernel, n_near, counts_of(late), len(held)), "away_group",
                    meta, away_size, units, flat(near, "any") + flat(late, "vmem") + held, kept_outs,
                    level_landing + full, share(model), LIM,
                )
            )
    everyone = rows * n_dp
    grad_in, grad_out = run_kernel(
        functools.partial(last_kernel, n_near, counts_of(late), len(held), len(past)), "last_group", meta, size, units,
        flat(near, "whole") + flat(late, "vmem") + held
        + [pair for kept in past for pair in zip(kept, ("cols", "cols", "whole", "whole"))],
        [((own, units), f32, "cols"), ((units, own), f32, "rows")],
        full + [
            pltpu.VMEM((rows, own), bf16),
            pltpu.VMEM((everyone, own), bf16),
            pltpu.VMEM((own, everyone), bf16),
            pltpu.VMEM((everyone, size), bf16),
            pltpu.VMEM((everyone, size), bf16),
        ],
        share(model) + 4 * everyone * own * units,
        LIM,
    )
    if paired:
        swapped = [cross(after(part, past[-2][0]), swap(1)) for part in parts[1::2]]
        far = (after(swapped[1], past[-1][0]).astype(f32) + parts[2].astype(f32)).astype(bf16)
        sums = [parts[0], swapped[0], cross(far, swap(2))]
    else:
        sums = [lax.psum_scatter(parts[0], "tp", scatter_dimension=1, tiled=True)]
    mixed, grad_patches = pl.pallas_call(
        functools.partial(restore_kernel, len(sums)), name="restore_rows",
        out_shape=[jax.ShapeDtypeStruct((rows, width), bf16)] * 2,
        compiler_params=small,
    )(ordering[None, :], *[after(array, grad_in) for array in sums])
    return (mixed, grad_patches, grad_in, grad_out)


def solution(mesh):
    return jax.shard_map(
        shards,
        mesh=mesh,
        in_specs=(
            P(("rep", "dp"), "tp"),
            P(("rep", "dp")),
            P(None, "tp"),
            P("tp", None),
            P(("rep", "dp"), "tp"),
        ),
        out_specs=(
            P(("rep", "dp"), "tp"),
            P(("rep", "dp"), "tp"),
            P(("rep", "dp"), "tp"),
            P(("rep", "tp"), "dp"),
        ),
        check_vma=False,
    )
```
